512 devices in a mesh: resp: 64 (over x, z_lo, core), tp: 8 (over y, z_hi).
Axes of the slice: x: 4, y: 4, z: 16 (z_hi: 2, z_lo: 8; z = z_hi * 8 + z_lo), core: 2. Of those that a mesh axis runs over, the one named last changes fastest.
Arguments:
- queries: bfloat16 [16384, 8192], P(('resp', 'tp')), may hold values from -6 to 6
- keys: bfloat16 [16384, 1024], P(('resp', 'tp')), may hold values from -6 to 6
- values: bfloat16 [16384, 1024], P(('resp', 'tp')), may hold values from -6 to 6
- out_grad: bfloat16 [16384, 8192], P(('resp', 'tp')), may hold values from -6 to 6
- prefix_keys: bfloat16 [4096, 1024], P('resp', 'tp'), may hold values from -6 to 6
- prefix_values: bfloat16 [4096, 1024], P('resp', 'tp'), may hold values from -6 to 6
- lengths: int32 [128], P('resp'), may hold values from 1 to 128, 10240 in all
- prompt_of: int32 [128], P('resp'), may hold values from 0 to 7, as said below
Outputs:
- grad_queries: bfloat16 [16384, 8192], P(('resp', 'tp'))
- grad_keys: bfloat16 [16384, 1024], P(('resp', 'tp'))
- grad_values: bfloat16 [16384, 1024], P(('resp', 'tp'))
- grad_prefix_keys: bfloat16 [4096, 1024], P('resp', 'tp')
- grad_prefix_values: bfloat16 [4096, 1024], P('resp', 'tp')
The draws below stay inside these ranges and needn't reach their ends.
Inputs may be any that keep to these rules, and one draw needn't show every extreme that they name: `prompt_of`: every prompt is the prompt of exactly 16 responses. `lengths`: some response has all 128 slots live.
All inputs are finite; a program needn't handle non-finite values. No bound on the sum of `lengths` on one device may be relied on, other than what follows from the above.
Results may differ from the reference program's by a relative error of at most 0.011.
Values may be sent and summed in bfloat16 or wider, within the bound.
A program may use at most 64 MiB of HBM per device.

```python
import math
import jax
import jax.numpy as jnp
import numpy as np
from jax import lax

HEADS = 64
KVH = 8
HD = 128
GROUP = 16
RCAP = 128
PLEN = 512
RESPONSES = 128
PROMPTS = 8
TOKENS = 16384


def draw_prompt_of(key, part):
    key = jax.random.fold_in(key, 7)
    order = jax.random.permutation(key, jnp.arange(RESPONSES, dtype=jnp.int32))
    return (order // GROUP).astype(jnp.int32)


def level_of(key, shape, shards, smallest, top_value):
    def one(dim, parts):
        draws = jax.random.uniform(jax.random.fold_in(jax.random.fold_in(key, 6), dim), (parts,), jnp.float32, smallest / len(shards), top_value / len(shards))
        return jnp.repeat(jnp.exp(draws), shape[dim] // parts).reshape((-1,) + (1,) * (len(shape) - dim - 1))

    gain = one(*shards[0])
    for cut in shards[1:]:
        gain = gain * one(*cut)
    return gain


def split_up(number_of, total, reach, lean):
    portions = [(1 << 20) // math.isqrt(standing ** lean) + 1 for standing in range(2, number_of + 1)]
    rest, given = total - reach - (number_of - 1), [1] * (number_of - 1)
    while rest > 0:
        free = [i for i in range(number_of - 1) if given[i] < reach]
        whole, left = sum([portions[i] for i in free]), rest
        for i in free:
            more = min(reach - given[i], max(1, left * portions[i] // whole), rest)
            given[i] = given[i] + more
            rest = rest - more
    return np.array([reach] + given)


def uneven_parts(rng, count, total, bound, lean):
    if count == 2:
        one = jax.random.randint(rng, (), max(1, total - bound), min(bound, total - 1) + 1)
        return jnp.stack([one, total - one])
    sizes = jnp.asarray(split_up(count, total, bound, lean), jnp.int32)
    twos = (count - 1) // 2
    giver, taker = sizes[1:1 + 2 * twos:2], sizes[2:2 + 2 * twos:2]
    room = jnp.minimum(giver - 1, bound - taker)
    passed = jax.random.randint(jax.random.fold_in(rng, 1), (twos,), 0, 1 << 20) % (room + 1)
    sizes = sizes.at[1:1 + 2 * twos:2].set(giver - passed).at[2:2 + 2 * twos:2].set(taker + passed)
    return sizes[jax.random.permutation(jax.random.fold_in(rng, 2), count)]


def bell_draw(own_key, shape, spread, reach, shards=(), held_as=jnp.bfloat16):
    entries = jax.random.normal(own_key, shape, jnp.float32) * spread
    if len(shards) > 0:
        entries = level_of(own_key, shape, shards, -0.22, 0.18) * entries
    return jnp.clip(entries, min=-reach, max=reach).astype(held_as)


def setup_inputs(seed: int = 0) -> dict:
    arg_keys = jax.random.split(jax.random.key(seed), 9)
    return {
        "queries": bell_draw(arg_keys[0], (TOKENS, HEADS * HD), 1.0, 6.0, ((0, 512),)),
        "keys": bell_draw(arg_keys[1], (TOKENS, KVH * HD), 1.0, 6.0, ((0, 512),)),
        "values": bell_draw(arg_keys[2], (TOKENS, KVH * HD), 1.0, 6.0, ((0, 512),)),
        "out_grad": bell_draw(arg_keys[3], (TOKENS, HEADS * HD), 1.0, 6.0, ((0, 512),)),
        "prefix_keys": bell_draw(arg_keys[4], (PROMPTS * PLEN, KVH * HD), 1.0, 6.0, ((0, 64), (1, 8))),
        "prefix_values": bell_draw(arg_keys[5], (PROMPTS * PLEN, KVH * HD), 1.0, 6.0, ((0, 64), (1, 8))),
        "lengths": uneven_parts(arg_keys[6], RESPONSES, RESPONSES * RCAP * 5 // 8, RCAP, 1).astype(jnp.int32),
        "prompt_of": draw_prompt_of(jax.random.fold_in(arg_keys[8], 71), 0),
    }


def one_response(q, k, v, g, pk, pv, length):
    scale = 1.0 / math.sqrt(HD)
    rep = HEADS // KVH
    qf = q.reshape(RCAP, KVH, rep, HD).astype(jnp.float32)
    kf = k.reshape(RCAP, KVH, HD).astype(jnp.float32)
    vf = v.reshape(RCAP, KVH, HD).astype(jnp.float32)
    pkf = pk.reshape(PLEN, KVH, HD).astype(jnp.float32)
    pvf = pv.reshape(PLEN, KVH, HD).astype(jnp.float32)
    positions = jnp.arange(RCAP, dtype=jnp.int32)
    causal = positions[None, :] <= positions[:, None]
    live = positions < length
    s_pre = jnp.einsum('ighd,jgd->ghij', qf, pkf) * scale
    s_self = jnp.einsum('ighd,jgd->ghij', qf, kf) * scale
    s_self = jnp.where(causal, s_self, -jnp.inf)
    top = jnp.maximum(lax.optimization_barrier(jnp.max(s_pre, -1)), lax.optimization_barrier(jnp.max(s_self, -1)))
    e_pre = jnp.exp(s_pre - top[..., None])
    e_self = jnp.exp(s_self - top[..., None])
    total = lax.optimization_barrier(jnp.sum(e_pre, -1)) + lax.optimization_barrier(jnp.sum(e_self, -1))
    p_pre = e_pre / total[..., None]
    p_self = e_self / total[..., None]
    b_pre = p_pre.astype(jnp.bfloat16).astype(jnp.float32)
    b_self = p_self.astype(jnp.bfloat16).astype(jnp.float32)
    attn = jnp.einsum('ghij,jgd->ighd', b_pre, pvf) + jnp.einsum('ghij,jgd->ighd', b_self, vf)
    gm = jnp.where(live[:, None], g, jnp.zeros_like(g))
    gf = gm.reshape(RCAP, KVH, rep, HD).astype(jnp.float32)
    delta = jnp.transpose(lax.optimization_barrier(jnp.sum(gf * attn, -1)), (1, 2, 0))
    dp_pre = jnp.einsum('ighd,jgd->ghij', gf, pvf)
    dp_self = jnp.einsum('ighd,jgd->ghij', gf, vf)
    ds_pre = (p_pre * (dp_pre - delta[..., None])).astype(jnp.bfloat16).astype(jnp.float32)
    ds_self = (p_self * (dp_self - delta[..., None])).astype(jnp.bfloat16).astype(jnp.float32)
    dq = (jnp.einsum('ghij,jgd->ighd', ds_pre, pkf) + jnp.einsum('ghij,jgd->ighd', ds_self, kf)) * scale
    dk = jnp.einsum('ghij,ighd->jgd', ds_self, qf) * scale
    dv = jnp.einsum('ghij,ighd->jgd', b_self, gf)
    dpk = jnp.einsum('ghij,ighd->jgd', ds_pre, qf) * scale
    dpv = jnp.einsum('ghij,ighd->jgd', b_pre, gf)
    return (dq.reshape(RCAP, HEADS * HD).astype(jnp.bfloat16), dk.reshape(RCAP, KVH * HD).astype(jnp.bfloat16), dv.reshape(RCAP, KVH * HD).astype(jnp.bfloat16), dpk.reshape(PLEN, KVH * HD), dpv.reshape(PLEN, KVH * HD))

def reference(queries, keys, values, out_grad, prefix_keys, prefix_values, lengths, prompt_of):
    qs = queries.reshape(RESPONSES, RCAP, HEADS * HD)
    ks = keys.reshape(RESPONSES, RCAP, KVH * HD)
    vs = values.reshape(RESPONSES, RCAP, KVH * HD)
    gs = out_grad.reshape(RESPONSES, RCAP, HEADS * HD)
    pks = prefix_keys.reshape(PROMPTS, PLEN, KVH * HD)
    pvs = prefix_values.reshape(PROMPTS, PLEN, KVH * HD)

    def step(carry, item):
        acc_k, acc_v = carry
        q, k, v, g, length, prompt = item
        pk = lax.dynamic_index_in_dim(pks, prompt, 0, keepdims=False)
        pv = lax.dynamic_index_in_dim(pvs, prompt, 0, keepdims=False)
        dq, dk, dv, dpk, dpv = one_response(q, k, v, g, pk, pv, length)
        acc_k = acc_k.at[prompt].add(dpk)
        acc_v = acc_v.at[prompt].add(dpv)
        return ((acc_k, acc_v), (dq, dk, dv))
    start = (jnp.zeros((PROMPTS, PLEN, KVH * HD), jnp.float32), jnp.zeros((PROMPTS, PLEN, KVH * HD), jnp.float32))
    (acc_k, acc_v), (dq, dk, dv) = lax.scan(step, start, (qs, ks, vs, gs, lengths.astype(jnp.int32), prompt_of.astype(jnp.int32)))
    return (dq.reshape(TOKENS, HEADS * HD), dk.reshape(TOKENS, KVH * HD), dv.reshape(TOKENS, KVH * HD), acc_k.reshape(PROMPTS * PLEN, KVH * HD).astype(jnp.bfloat16), acc_v.reshape(PROMPTS * PLEN, KVH * HD).astype(jnp.bfloat16))
```

```python
import functools
import math

import jax
import jax.numpy as jnp
from jax import lax
from jax.experimental import pallas as pl
from jax.experimental.pallas import tpu as pltpu
from jax.sharding import PartitionSpec as P

HD = 128
RCAP = 128
PLEN = 512
PROMPTS = 8
X, Y, ZL, C, ZH = 4, 4, 8, 2, 2
Z = ZL * ZH
REP = 8
QW = REP * HD
LATE = 6
TOK = 32
MESH = pl.DeviceIdType.MESH
F32 = jnp.float32
BF16 = jnp.bfloat16
SCALE = 1.0 / math.sqrt(HD)
SCALE2 = SCALE * math.log2(math.e)


def where_is(x, y, z, c):
    return {"resp": x * (ZL * C) + lax.rem(z, ZL) * C + c, "tp": y * ZH + z // ZL}


def remote(src, dst, send, recv, device):
    return pltpu.make_async_remote_copy(
        src_ref=src, dst_ref=dst, send_sem=send, recv_sem=recv, device_id=device, device_id_type=MESH
    )


def dot_nt(a, b):
    return lax.dot_general(a, b, (((1,), (1,)), ((), ())), preferred_element_type=F32)


def dot_nn(a, b):
    return lax.dot_general(a, b, (((1,), (0,)), ((), ())), preferred_element_type=F32)


def dot_tn(a, b):
    return lax.dot_general(a, b, (((0,), (0,)), ((), ())), preferred_element_type=F32)


ROWS = REP * TOK
CHUNK = 128
CHUNKS = (PLEN + RCAP) // CHUNK


def kernel(
    q_in, k_in, v_in, g_in, pk_in, pv_in, len_in, prompt_in,
    dq_out, dkvr, zr,
    len_s, prompt_s, aux_l, aux_v, aux_s, qs, gs, ks, vs, side, kvrel, rows, kvx, pkb, pvb,
    term, dense, dqs, dkvs, dkrel,
    ra, rb, ra1, rb1, ra2, rb2, xsum, zrel, qh, gh, kk, vv, s_scr, dp_scr, p_scr, b_scr, ds_scr,
    aux_sem, in_sem, r_ss, r_rs, kr_ss, kr_rs, kx_ss, kx_rs,
    near_in, far_in, p_ss, p_rs, z_ss, z_rs, x_ss, x_rs, x2_ss, x2_rs,
    dq_ss, dq_rs, dkv_ss, dkv_rs, dr_ss, dr_rs, df_ss, df_rs,
    rx_ss, rx_rs, rx2_ss, rx2_rs, rz_ss, rz_rs, rl_rs,
):
    r = lax.axis_index("resp")
    t = lax.axis_index("tp")
    x, zl, c = r // (ZL * C), lax.rem(r // C, ZL), lax.rem(r, C)
    y, zh = t // ZH, lax.rem(t, ZH)
    z = zh * ZL + zl
    head = y * C + c
    xr, xl = lax.rem(x + 1, X), lax.rem(x + X - 1, X)
    xo = lax.rem(x + 2, X)
    zr_, zl_ = lax.rem(z + 1, Z), lax.rem(z + Z - 1, Z)
    here = where_is(x, y, z, c)

    z4 = (lax.rem(z + 4, Z), lax.rem(z + Z - 4, Z))
    y_odd = lax.rem(y, 2) == 1

    loads = [
        pltpu.make_async_copy(k_in, ks, in_sem.at[0]),
        pltpu.make_async_copy(v_in, vs, in_sem.at[1]),
        pltpu.make_async_copy(q_in, qs, in_sem.at[2]),
        pltpu.make_async_copy(g_in, gs, in_sem.at[3]),
    ]
    for cp in loads:
        cp.start()
    ints = [
        pltpu.make_async_copy(len_in, len_s, aux_sem.at[0]),
        pltpu.make_async_copy(prompt_in, prompt_s, aux_sem.at[3]),
    ]
    for cp in ints:
        cp.start()

    barrier = pltpu.get_barrier_semaphore()

    def greet(x_, y_, z_, c_):
        pl.semaphore_signal(barrier, inc=1, device_id=where_is(x_, y_, z_, c_), device_id_type=MESH)

    def greet_y(i, carry):
        y_ = lax.rem(y + i, Y)
        greet(x, y_, z, c)
        greet(x, y_, z, 1 - c)
        return carry

    lax.fori_loop(1, Y, greet_y, 0)
    greet(xr, y, z, c)
    greet(xl, y, z, c)
    greet(xo, y, z, c)
    greet(x, y, z, 1 - c)
    z2 = (lax.rem(z + 2, Z), lax.rem(z + Z - 2, Z))
    for z_ in (zr_, zl_) + z2:
        greet(x, y, z_, c)
        greet(x, y, z_, 1 - c)

    def tell(sem):
        for i in (0, 1):
            pl.semaphore_signal(sem.at[i], inc=1, device_id=where_is(x, y, z2[i], c), device_id_type=MESH)

    def told(sem):
        for i in (0, 1):
            pl.semaphore_wait(sem.at[i], 1)

    for cp in loads:
        cp.wait()
    for h in range(8):
        side[h, :, :QW] = qs[:, h * QW : (h + 1) * QW]
        side[h, :, QW : 2 * QW] = gs[:, h * QW : (h + 1) * QW]
        side[h, :, 2 * QW : 2 * QW + HD] = ks[:, h * HD : (h + 1) * HD]
        side[h, :, 2 * QW + HD :] = vs[:, h * HD : (h + 1) * HD]

    pl.semaphore_wait(barrier, 2 * (Y - 1) + 3 + 1 + 8)
    tell(near_in)

    def chunk(w, x_, zl_src):
        return prefix[w].at[x_ * 2 + zl_src // 4, lax.rem(zl_src, 4)]

    own_core = c == zh
    prefix_in = (pk_in, pv_in)
    prefix = (pkb, pvb)

    def mine_near(w):
        return pltpu.make_async_copy(prefix_in[w], chunk(w, x, zl).at[c], p_ss.at[w, 0])

    def mine_far(w, i):
        z_ = (z, zr_, z2[0], zl_, z2[1])[i]
        ref = chunk(w, x, zl).at[c]
        return remote(prefix_in[w], ref, p_ss.at[w, i], p_rs.at[w, zl, c], where_is(x, y, z_, zh))

    def mine_send(w):
        for i in (2, 4, 1, 3):
            mine_far(w, i).start()

        @pl.when(own_core)
        def _():
            mine_near(w).start()

        @pl.when(jnp.logical_not(own_core))
        def _():
            mine_far(w, 0).start()

    def halves_wait(w, s):
        for half in (0, 1):
            ref = chunk(w, x, s).at[half]
            remote(prefix_in[w], ref, p_ss.at[w, 0], p_rs.at[w, s, half], here).wait_recv()

    def mine_wait(w):
        @pl.when(own_core)
        def _():
            mine_near(w).wait()
            remote(prefix_in[w], chunk(w, x, zl).at[1 - c], p_ss.at[w, 0], p_rs.at[w, zl, 1 - c], here).wait_recv()

    mine_send(0)
    mine_send(1)

    def slot_of(y_, c_):
        return ((y_ // 2) * 2 + c_) * 2 + lax.rem(y_, 2)

    my_slot = slot_of(y, c)

    def row_copy(dy, dc):
        y_, c_ = lax.rem(y + dy, Y), lax.rem(c + dc, C)
        return remote(
            side.at[y_ * C + c_], rows.at[my_slot], r_ss.at[dy * 2 + dc], r_rs.at[my_slot], where_is(x, y_, z, c_)
        )

    def unseen(zh_src, odd):
        return jnp.logical_and(zh_src == 1, odd)

    def rel_copy(kv, way):
        src = side.at[pl.ds(4 * way, 4), :, pl.ds(2 * QW + kv * HD, HD)]
        return remote(src, kvrel.at[kv, way], kr_ss.at[kv, way], kr_rs.at[kv, way], where_is(x, y, z4[way], c))

    def rel_src(way):
        return z4[1 - way] // ZL

    def rel_on(kv, way):
        return [
            remote(
                kvrel.at[kv, way, i],
                kvx.at[kv, my_slot],
                kx_ss.at[kv, way * 4 + i],
                kx_rs.at[kv, my_slot],
                where_is(x, 2 * way + i // 2, z4[way], i % 2),
            )
            for i in range(4)
        ]

    def rel_start(kv):
        @pl.when(jnp.logical_not(unseen(zh, y_odd)))
        def _():
            for way in (0, 1):
                rel_copy(kv, way).start()

    def rel_pass(kv):
        for way in (0, 1):

            @pl.when(jnp.logical_not(unseen(rel_src(way), y_odd)))
            def _():
                rel_copy(kv, way).wait_recv()
                for cp in rel_on(kv, way):
                    cp.start()

    def kvx_wait(kv):
        for y_ in range(Y):
            for c_ in range(C):

                @pl.when(jnp.logical_not(unseen(1 - zh, y_ % 2 == 1)))
                def _():
                    ref = kvx.at[kv, slot_of(y_, c_)]
                    remote(ref, ref, kx_ss.at[kv, 0], kx_rs.at[kv, slot_of(y_, c_)], here).wait_recv()

    far = [(dy, dc) for dc in (0, 1) for dy in (1, 3, 2, 0) if (dy, dc) != (0, 0)]

    def y_start(*pairs):
        for dy, dc in pairs:
            row_copy(dy, dc).start()

    y_start((1, 0), (3, 0))

    @pl.when(jnp.logical_not(own_core))
    def _():
        y_start((2, 0), (1, 1), (3, 1), (2, 1), (0, 1))

    own = pltpu.make_async_copy(side.at[head], rows.at[my_slot], r_ss.at[0])
    own.start()

    for cp in ints:
        cp.wait()
    lane = lax.broadcasted_iota(jnp.int32, (8, 128), 1)
    aux_l[...] = jnp.where(
        lane == 0,
        prompt_s[0],
        jnp.where(lane == 1, prompt_s[1], jnp.where(lane == 2, len_s[0], len_s[1])),
    )
    aux_own = pltpu.make_async_copy(aux_l, aux_v.at[c], aux_sem.at[0])
    aux_own.start()
    aux_far = remote(aux_l, aux_v.at[c], aux_sem.at[1], aux_sem.at[2], where_is(x, y, z, 1 - c))
    aux_far.start()

    def z_copy(w, way, far_, s):
        up_dev = where_is(x, y, lax.rem(z + 1 + far_, Z), c)
        down_dev = where_is(x, y, lax.rem(z + Z - 1 - far_, Z), c)
        ref = chunk(w, x, s)
        return remote(ref, ref, z_ss.at[w, way, far_, s], z_rs.at[w, s], up_dev if way == 0 else down_dev)

    def x_copy(w, way, s):
        ref, dev = chunk(w, x, s), where_is(xr if way == 0 else xl, y, z, c)
        return remote(ref, ref, x_ss.at[w, way, s], x_rs.at[w, way, s], dev)

    def x_arrived(w, way, s):
        ref = chunk(w, xl if way == 0 else xr, s)
        return remote(ref, ref, x_ss.at[w, way, s], x_rs.at[w, way, s], here)

    def x2_copy(w, way, s):
        ref, dev = chunk(w, xl if way == 0 else xr, s).at[way], where_is(xr if way == 0 else xl, y, z, c)
        return remote(ref, ref, x2_ss.at[w, way, s], x2_rs.at[w, way, s], dev)

    def x3_copy(w, s):
        ref = chunk(w, x, s)
        return remote(ref, ref, x2_ss.at[w, 0, s], x2_rs.at[w, 0, s], where_is(xo, y, z, c))

    def x3_arrived(w, s):
        ref = chunk(w, xo, s)
        return remote(ref, ref, x2_ss.at[w, 0, s], x2_rs.at[w, 0, s], here)

    def x2_arrived(w, way, s):
        ref = chunk(w, xo, s).at[way]
        return remote(ref, ref, x2_ss.at[w, way, s], x2_rs.at[w, way, s], here)

    def source(way, k):
        s = lax.rem(z + (Z - k if way == 0 else k), Z)
        return s // ZL == c, lax.rem(s, ZL)

    def x_start(w, s):
        x_copy(w, 0, s).start()
        x_copy(w, 1, s).start()

    def forwards(w, way, j, s):
        return [z_copy(w, way, i, s) for i in (2, 1, 0) if not (j == 2 and way == 1 and i == 2)]

    def stop(w, j):
        for way in (0, 1):
            live, s = source(way, 3 * j - 1 if j else 0)

            @pl.when(live)
            def _():
                if j == 1:
                    halves_wait(w, s)
                elif j == 2:
                    z_copy(w, way, 0, s).wait_recv()
                if j > 0:
                    for cp in forwards(w, way, j, s):
                        cp.start()

        for way in (0, 1):
            live, s = source(way, 3 * j - 1 if j else 0)

            @pl.when(live)
            def _():
                if j > 0 or way == 0:
                    x_start(w, s)

        for k in ((), (1,), (3, 4))[j]:
            for way in (0, 1):
                arrive(w, way, k)

    def arrive(w, way, k):
        live, s = source(way, k)

        @pl.when(live)
        def _():
            if k == 1:
                halves_wait(w, s)
            else:
                z_copy(w, way, 0, s).wait_recv()
            x_start(w, s)
            if k >= LATE:
                x3_copy(w, s).start()

    def stop_sent(w, j):
        for way in (0, 1):
            live, s = source(way, 3 * j - 1)

            @pl.when(live)
            def _():
                for cp in forwards(w, way, j, s):
                    cp.wait_send()

    def last_arrivals(w):
        for way, k in ((0, 6), (1, 6), (0, 7), (1, 7), (0, 8)):
            arrive(w, way, k)

    def pass_on(w, way, k):
        live, s = source(way, k)

        @pl.when(live)
        def _():
            for x_way in (0, 1):
                x_arrived(w, x_way, s).wait_recv()
                x2_copy(w, x_way, s).start()

    def all_on(w, low, high):
        for k in range(low, high):
            pass_on(w, 0, k)
            if 0 < k < 8:
                pass_on(w, 1, k)

    all_sources = [(way, k) for k in range(9) for way in (0, 1) if way == 0 or 0 < k < 8]

    def x2_wait(w):
        for way, k in all_sources:
            live, s = source(way, k)

            @pl.when(live)
            def _():
                if k >= LATE:
                    x_arrived(w, 0, s).wait_recv()
                    x_arrived(w, 1, s).wait_recv()
                    x3_arrived(w, s).wait_recv()
                else:
                    x2_arrived(w, 0, s).wait_recv()
                    x2_arrived(w, 1, s).wait_recv()

    def y_between(*pairs):
        @pl.when(own_core)
        def _():
            y_start(*pairs)

    mine_wait(0)
    stop(0, 0)
    y_between((2, 0), (1, 1), (3, 1))
    mine_wait(1)
    told(near_in)
    tell(far_in)
    stop(0, 1)
    stop(1, 0)
    told(far_in)
    rel_start(0)
    y_between((2, 1), (0, 1))
    stop(0, 2)
    stop(1, 1)
    rel_pass(0)
    rel_start(1)
    last_arrivals(0)
    stop(1, 2)
    rel_pass(1)
    all_on(0, 0, LATE)
    last_arrivals(1)

    for dy, dc in far:
        ref = rows.at[slot_of(lax.rem(y + dy, Y), lax.rem(c + dc, C))]
        remote(ref, ref, r_ss.at[0], r_rs.at[slot_of(lax.rem(y + dy, Y), lax.rem(c + dc, C))], here).wait_recv()
    kvx_wait(0)
    own.wait()
    aux_own.wait()
    remote(aux_l, aux_v.at[1 - c], aux_sem.at[1], aux_sem.at[2], here).wait_recv()

    to_smem = pltpu.make_async_copy(aux_v, aux_s, aux_sem.at[3])
    to_smem.start()
    to_smem.wait()

    x2_wait(0)

    def q_cols(ref, h):
        return ref.at[:, pl.ds(pl.multiple_of(h * QW, QW), QW)]

    def dq_copy(sl):
        rho = sl // 2
        y_, c_ = (rho // 2) * 2 + lax.rem(sl, 2), lax.rem(rho, 2)
        dst = q_cols(dq_out, head)
        return (
            sl == my_slot,
            remote(dqs.at[sl], dst, dq_ss.at[sl], dq_rs.at[head], where_is(x, y_, z, c_)),
            pltpu.make_async_copy(dqs.at[sl], dst, dq_ss.at[sl]),
        )

    def dkv_copy(rho, yb):
        y_, c_ = (rho // 2) * 2 + yb, lax.rem(rho, 2)
        i = dk_slot(rho, yb)
        src, dst = dkvs.at[zh, i], dkvr.at[zh, head]
        return (
            jnp.logical_and(y_ == y, c_ == c),
            remote(src, dst, dkv_ss.at[i], dkv_rs.at[zh * 8 + head], where_is(x, y_, z, c_)),
            pltpu.make_async_copy(src, dst, dkv_ss.at[i]),
        )

    def dk_slot(rho, yb):
        return (rho // 2) * 4 + yb * 2 + lax.rem(rho, 2)

    def drel_copy(kv, way, yb):
        dev = where_is(x, y, jnp.where(way == 0, z4[0], z4[1]), c)
        src = dkvs.at[1 - zh, pl.ds(way * 4 + yb * 2, 2), kv]
        return remote(src, dkrel.at[kv, way, yb], dr_ss.at[kv, way, yb], dr_rs.at[kv, way, yb], dev)

    def drel_start(kv, way):
        drel_copy(kv, way, 0).start()

        @pl.when(zh == 1)
        def _():
            drel_copy(kv, way, 1).start()

    def drel_on(kv, way, yb):
        zs = rel_src(way)
        return [
            remote(
                dkrel.at[kv, way, yb, i],
                dkvr.at[zs, head, kv],
                df_ss.at[kv, way, yb * 2 + i],
                df_rs.at[kv, head],
                where_is(x, 2 * way + yb, z4[way], i),
            )
            for i in (0, 1)
        ]

    def drel_pass(kv, way):
        drel_copy(kv, way, 0).wait_recv()
        for cp in drel_on(kv, way, 0):
            cp.start()

        @pl.when(rel_src(way) == 1)
        def _():
            drel_copy(kv, way, 1).wait_recv()
            for cp in drel_on(kv, way, 1):
                cp.start()

    def send(copies):
        local, far_cp, near_cp = copies

        @pl.when(local)
        def _():
            near_cp.start()

        @pl.when(jnp.logical_not(local))
        def _():
            far_cp.start()

    def sent(copies):
        local, far_cp, near_cp = copies

        @pl.when(local)
        def _():
            near_cp.wait()

        @pl.when(jnp.logical_not(local))
        def _():
            far_cp.wait_send()

    def fold(a, op):
        return op(a.reshape(CHUNK // 8, 8, ROWS), 0)

    def keys_of(kv, prompt, rho, to):
        to[:PLEN] = prefix[kv][prompt].reshape(PLEN, HD)
        for b in (0, 1):
            i = rho * 2 + b
            near = pl.ds(pl.multiple_of(PLEN + (2 * b + zh) * TOK, TOK), TOK)
            over = pl.ds(pl.multiple_of(PLEN + (2 * b + 1 - zh) * TOK, TOK), TOK)
            low = 2 * QW + kv * HD
            to[near] = rows[i, :, low : low + HD]
            crossed = kvx[kv, i].astype(F32)
            if b == 1:
                crossed = jnp.where(zh == 1, crossed, 0.0)
            to[over] = crossed.astype(BF16)

    def leave(kv, rho, grad):
        for i in range(4):
            for ct in (0, 1):
                low = (i * 2 + ct) * 64
                term[kv, rho, ct, i] = grad[low : low + 64].astype(BF16)
        for tb in range(4):
            low = PLEN + tb * TOK
            dkvs[tb % 2, dk_slot(rho, tb // 2), kv] = grad[low : low + TOK].astype(BF16)

    def weigh(rho, carry):
        prompt = aux_s[lax.rem(rho, 2), 0, rho // 2]
        length = aux_s[lax.rem(rho, 2), 0, 2 + rho // 2]
        k_rho = kk.at[rho]
        keys_of(0, prompt, rho, k_rho)
        acc = []
        for b in (0, 1):
            i = rho * 2 + b
            qa, ga = rows[i, :, :QW], rows[i, :, QW : 2 * QW]
            tok = lax.broadcasted_iota(jnp.int32, (TOK, HD), 0) + (64 * b + TOK * zh)
            keep = jnp.where(tok < length, 1.0, 0.0)
            q = jnp.concatenate([qa[:, h * HD : (h + 1) * HD] for h in range(REP)], axis=0)
            g = jnp.concatenate(
                [(ga[:, h * HD : (h + 1) * HD].astype(F32) * keep).astype(BF16) for h in range(REP)], axis=0
            )
            qh[i] = q
            gh[i] = g
            top = jnp.full((8, ROWS), -jnp.inf, F32)
            for n in range(CHUNKS):
                at = slice(n * CHUNK, (n + 1) * CHUNK)
                s = dot_nt(k_rho[at], q)
                if n == CHUNKS - 1:
                    col = lax.broadcasted_iota(jnp.int32, (CHUNK, ROWS), 1)
                    key = lax.broadcasted_iota(jnp.int32, (CHUNK, ROWS), 0)
                    s = jnp.where(key <= lax.rem(col, TOK) + (64 * b + TOK * zh), s, -jnp.inf)
                s_scr[b, at] = s
                top = jnp.maximum(top, fold(s, jnp.max))
            top = jnp.max(top, 0, keepdims=True)
            total = jnp.zeros((8, ROWS), F32)
            for n in range(CHUNKS):
                at = slice(n * CHUNK, (n + 1) * CHUNK)
                e = jnp.exp2((s_scr[b, at] - top) * SCALE2)
                s_scr[b, at] = e
                total = total + fold(e, jnp.sum)
            inv = 1.0 / jnp.sum(total, 0, keepdims=True)
            for n in range(CHUNKS):
                at = slice(n * CHUNK, (n + 1) * CHUNK)
                p = s_scr[b, at] * inv
                p_scr[i, at] = p
                b_scr[b, at] = p.astype(BF16)
            acc.append(dot_nn(b_scr[b], g))
        leave(1, rho, acc[0] + acc[1])

        @pl.when(lax.rem(rho, 2) == 1)
        def _():
            drel_start(1, rho // 2)

        @pl.when(rho == 0)
        def _():
            all_on(1, 0, 3)

        @pl.when(rho == 1)
        def _():
            all_on(1, 3, LATE)

        return carry

    def differentiate(rho, carry):
        prompt = aux_s[lax.rem(rho, 2), 0, rho // 2]
        keys_of(1, prompt, rho, vv)
        acc = []
        for b in (0, 1):
            i = rho * 2 + b
            mixed = jnp.zeros((8, ROWS), F32)
            for n in range(CHUNKS):
                at = slice(n * CHUNK, (n + 1) * CHUNK)
                dp = dot_nt(vv[at], gh[i])
                dp_scr[b, at] = dp
                mixed = mixed + fold(p_scr[i, at] * dp, jnp.sum)
            delta = jnp.sum(mixed, 0, keepdims=True)
            for n in range(CHUNKS):
                at = slice(n * CHUNK, (n + 1) * CHUNK)
                ds_scr[i, at] = (p_scr[i, at] * (dp_scr[b, at] - delta)).astype(BF16)
            acc.append(dot_nn(ds_scr[i], qh[i]))
        leave(0, rho, (acc[0] + acc[1]) * SCALE)

        @pl.when(lax.rem(rho, 2) == 1)
        def _():
            drel_start(0, rho // 2)

        for b in (0, 1):
            send(dkv_copy(rho, b))

        @pl.when(rho == 2)
        def _():
            for way in (0, 1):
                drel_pass(1, way)

        first(1, order(rho))

        @pl.when(rho >= 2)
        def _():
            second(1, order(rho - 2))

        return carry

    def query_grads(rho, carry):
        for b in (0, 1):
            i = rho * 2 + b
            dq = (dot_tn(kk[rho], ds_scr[i]) * SCALE).T.astype(BF16)
            for h in range(REP):
                dqs[i, :, h * HD : (h + 1) * HD] = dq[h * TOK : (h + 1) * TOK]
            send(dq_copy(i))
        return carry

    def part(w, x_, n, half):
        return dense.at[w, x_ * 2 + n // 2, half, pl.ds(lax.rem(n, 2) * 2, 2)]

    def own_part(w, x_, n, half):
        return dense[w, x_ * 2 + n // 2, half, pl.ds(lax.rem(n, 2) * 2, 2)].astype(F32)

    def rx_copy(w, way, n):
        if way == 0:
            src, dst, dev = part(w, xo, n, 0), ra.at[w, n], where_is(xr, y, z, c)
        elif way == 1:
            src, dst, dev = part(w, xo, n, 1), rb.at[w, n], where_is(xl, y, z, c)
        elif way == 2:
            src, dst, dev = part(w, xr, n, 1), rb1.at[w, n], where_is(xr, y, z, c)
        else:
            src, dst, dev = part(w, xl, n, 0), ra1.at[w, n], where_is(xl, y, z, c)
        return remote(src, dst, rx_ss.at[w, way, n], rx_rs.at[w, way, n], dev)

    def rx2_copy(w, way, n):
        if way == 0:
            src, dst, dev = ra.at[w, n], ra2.at[w, n], where_is(xr, y, z, c)
        else:
            src, dst, dev = rb.at[w, n], rb2.at[w, n], where_is(xl, y, z, c)
        return remote(src, dst, rx2_ss.at[w, way, n], rx2_rs.at[w, way, n], dev)

    rising = (zh != c) == (zl < 4)

    def order(i):
        n = lax.rem(i, 2) * 2 + i // 2
        return jnp.where(rising, n, 3 - n)

    def spread_all(w):
        def spread_half(i, carry):
            ip = jnp.where(rising, i, 1 - i)
            two = pl.ds(ip * 2, 2)

            def spread(p, carry):
                acc = jnp.zeros((2, 2, 64, HD), F32)
                for rho in range(4):
                    hit = aux_s[rho % 2, 0, rho // 2] == p
                    acc = acc + jnp.where(hit, term[w, rho, :, two].astype(F32), 0.0)
                dense[w, p, :, two] = acc.astype(BF16)
                return carry

            lax.fori_loop(0, PROMPTS, spread, 0)
            for j in (0, 1):
                for way in (0, 1):
                    rx_copy(w, way, order(2 * i + j)).start()
            return carry

        lax.fori_loop(0, 2, spread_half, 0)

    def z_dist(zt):
        return lax.rem(c * ZL + zt - z + 23, Z) - 7

    def z_direct(w, zt, ct, d):
        src, dst, zd = xsum.at[w, zt, ct], zr.at[w, d + 4], c * ZL + zt
        return (
            jnp.logical_and(d == 0, ct == c),
            remote(src, dst, rz_ss.at[w, ct, zt], rz_rs.at[w, d + 4], where_is(x, y, zd, ct)),
            pltpu.make_async_copy(src, dst, rz_ss.at[w, ct, zt]),
        )

    def z_stop(w, zt, d):
        up_ = d > 0
        zd = lax.rem(z + Z + jnp.where(up_, d - 4, d + 4), Z)
        i = jnp.where(up_, d, -d) - 5
        return remote(xsum.at[w, zt], zrel.at[w, i], rz_ss.at[w, 0, zt], rl_rs.at[w, i], where_is(x, y, zd, c))

    def is_far(d):
        return jnp.logical_or(d > 4, d < -4)

    def is_near(d):
        return jnp.logical_and(d < 4, d > -4)

    def first(w, n):
        rx_copy(w, 0, n).wait_recv()
        ra[w, n] = (ra[w, n].astype(F32) + own_part(w, xr, n, 0)).astype(BF16)
        rx2_copy(w, 0, n).start()
        rx_copy(w, 2, n).start()
        rx_copy(w, 1, n).wait_recv()
        rb[w, n] = (rb[w, n].astype(F32) + own_part(w, xl, n, 1)).astype(BF16)
        rx2_copy(w, 1, n).start()
        rx_copy(w, 3, n).start()

    def second(w, n):
        rx_copy(w, 3, n).wait_recv()
        rx2_copy(w, 0, n).wait_recv()
        one = own_part(w, x, n, 0) + ra1[w, n].astype(F32) + ra2[w, n].astype(F32)
        rx_copy(w, 2, n).wait_recv()
        rx2_copy(w, 1, n).wait_recv()
        two = own_part(w, x, n, 1) + rb1[w, n].astype(F32) + rb2[w, n].astype(F32)
        for i in (0, 1):
            zt = 2 * n + i
            xsum[w, zt, 0] = one[i].astype(BF16)
            xsum[w, zt, 1] = two[i].astype(BF16)
            d = z_dist(zt)

            @pl.when(is_near(d))
            def _():
                for ct in (0, 1):
                    send(z_direct(w, zt, ct, d))

            @pl.when(is_far(d))
            def _():
                z_stop(w, zt, d).start()

    zt_stop = lax.rem(zl + 4, ZL)
    d_stop = z_dist(zt_stop)

    def stop_sum(w):
        def stop_wait(i, carry):
            @pl.when(jnp.logical_or(i < 3, d_stop > 0))
            def _():
                remote(zrel.at[w, i], zrel.at[w, i], rz_ss.at[w, 0, 0], rl_rs.at[w, i], here).wait_recv()

            return carry

        lax.fori_loop(0, 4, stop_wait, 0)
        for ct in (0, 1):
            three = xsum[w, zt_stop, ct].astype(F32)
            for i in range(3):
                three = three + zrel[w, i, ct].astype(F32)

            @pl.when(d_stop > 0)
            def _():
                xsum[w, zt_stop, ct] = (three + zrel[w, 3, ct].astype(F32)).astype(BF16)

            @pl.when(d_stop < 0)
            def _():
                xsum[w, zt_stop, ct] = three.astype(BF16)

            z_direct(w, zt_stop, ct, d_stop)[1].start()

    lax.fori_loop(0, 4, weigh, 0)
    spread_all(1)
    x2_wait(1)
    kvx_wait(1)
    lax.fori_loop(0, 4, differentiate, 0)
    spread_all(0)
    drel_pass(0, 0)
    lax.fori_loop(0, 4, query_grads, 0)
    second(1, order(2))
    second(1, order(3))

    def last(i, carry):
        @pl.when(i < 4)
        def _():
            first(0, order(i))

        @pl.when(i == 1)
        def _():
            drel_pass(0, 1)

        @pl.when(i == 2)
        def _():
            stop_sum(1)

        @pl.when(i >= 1)
        def _():
            second(0, order(i - 1))

        return carry

    lax.fori_loop(0, 5, last, 0)
    stop_sum(0)

    def dkv_wait(h, carry):
        near = dkvr.at[zh, h]

        @pl.when(h != head)
        def _():
            remote(near, near, dkv_ss.at[0], dkv_rs.at[zh * 8 + h], here).wait_recv()

        @pl.when(jnp.logical_not(unseen(zh, y_odd)))
        def _():
            for kv in (0, 1):
                over = dkvr.at[1 - zh, h, kv]
                remote(over, over, dkv_ss.at[0], df_rs.at[kv, h], here).wait_recv()

        return carry

    def dkv_sent(i, carry):
        for yb in (0, 1):
            sent(dkv_copy(i, yb))
        return carry

    lax.fori_loop(0, 4, dkv_sent, 0)
    lax.fori_loop(0, 8, dkv_wait, 0)
    def z_sent(i, carry):
        w, n = i // ZL, lax.rem(i, ZL)
        d = z_dist(n)

        @pl.when(is_far(d))
        def _():
            z_stop(w, n, d).wait_send()

        @pl.when(jnp.logical_not(is_far(d)))
        def _():
            for ct in (0, 1):
                sent(z_direct(w, n, ct, d))

        return carry

    def z_wait(i, carry):
        for w in (0, 1):

            @pl.when(jnp.logical_not(jnp.logical_and(own_core, i == 4)))
            def _():
                remote(zr.at[w, i], zr.at[w, i], rz_ss.at[w, 0, 0], rz_rs.at[w, i], here).wait_recv()

        return carry

    lax.fori_loop(0, 2 * ZL, z_sent, 0)
    lax.fori_loop(0, 9, z_wait, 0)

    def dq_wait(h, carry):
        @pl.when(h != head)
        def _():
            ref = q_cols(dq_out, h)
            remote(ref, ref, dq_ss.at[0], dq_rs.at[h], here).wait_recv()

        return carry

    def dq_sent(i, carry):
        sent(dq_copy(i))
        return carry

    lax.fori_loop(0, 8, dq_sent, 0)
    lax.fori_loop(0, 8, dq_wait, 0)
    aux_far.wait_send()
    for dy, dc in far:
        row_copy(dy, dc).wait_send()

    @pl.when(jnp.logical_not(unseen(zh, y_odd)))
    def _():
        for kv in (0, 1):
            for way in (0, 1):
                rel_copy(kv, way).wait_send()

    for way in (0, 1):

        @pl.when(jnp.logical_not(unseen(rel_src(way), y_odd)))
        def _():
            for cp in rel_on(0, way) + rel_on(1, way):
                cp.wait_send()

        for kv in (0, 1):
            drel_copy(kv, way, 0).wait_send()
            for cp in drel_on(kv, way, 0):
                cp.wait_send()

        @pl.when(zh == 1)
        def _():
            for kv in (0, 1):
                drel_copy(kv, way, 1).wait_send()

        @pl.when(rel_src(way) == 1)
        def _():
            for kv in (0, 1):
                for cp in drel_on(kv, way, 1):
                    cp.wait_send()

    for w in (0, 1):
        for i in (1, 2, 3, 4):
            mine_far(w, i).wait_send()

        @pl.when(jnp.logical_not(own_core))
        def _():
            mine_far(w, 0).wait_send()

    for w in (0, 1):
        for j in (1, 2):
            stop_sent(w, j)

    def x_sent(s, carry):
        for w in (0, 1):
            for way in (0, 1):
                x_copy(w, way, s).wait_send()
        return carry

    lax.fori_loop(0, ZL, x_sent, 0)
    for w in (0, 1):
        for way, k in all_sources:
            live, s = source(way, k)

            @pl.when(live)
            def _():
                if k >= LATE:
                    x3_copy(w, s).wait_send()
                else:
                    x2_copy(w, 0, s).wait_send()
                    x2_copy(w, 1, s).wait_send()

    def rx_sent(n, carry):
        for w in (0, 1):
            for way in range(4):
                rx_copy(w, way, n).wait_send()
            for way in (0, 1):
                rx2_copy(w, way, n).wait_send()
        return carry

    lax.fori_loop(0, 4, rx_sent, 0)


def finish(dq_in, dkvr_in, zr_in, dq_out, dk_out, dv_out, gpk_out, gpv_out, dq, dkvr, zr, sem):
    loads = [
        pltpu.make_async_copy(dq_in, dq, sem.at[0]),
        pltpu.make_async_copy(dkvr_in, dkvr, sem.at[1]),
        pltpu.make_async_copy(zr_in, zr, sem.at[2]),
    ]
    for cp in loads:
        cp.start()
    loads[0].wait()
    store = pltpu.make_async_copy(dq, dq_out, sem.at[3])
    store.start()
    loads[1].wait()
    loads[2].wait()
    t = lax.axis_index("tp")
    near = lax.rem(t, ZH)
    whole = jnp.where(jnp.logical_and(near == 1, lax.rem(t // ZH, 2) == 1), 0, 1)
    for h in range(8):
        over = jnp.where(whole == 1, dkvr[1 - near, h].astype(F32), 0.0)
        summed = dkvr[near, h].astype(F32) + over
        dk_out[:, h * HD : (h + 1) * HD] = summed[0].astype(BF16)
        dv_out[:, h * HD : (h + 1) * HD] = summed[1].astype(BF16)
    for w, ref in ((0, gpk_out), (1, gpv_out)):
        all_z = zr[w, 0].astype(F32)
        for i in range(1, 9):
            all_z = all_z + zr[w, i].astype(F32)
        ref[...] = all_z.astype(BF16)
    store.wait()


def body(queries, keys, values, out_grad, prefix_keys, prefix_values, lengths, prompt_of):
    dma = pltpu.SemaphoreType.DMA
    vm = lambda *shape: pltpu.VMEM(shape, BF16)
    out = lambda *shape: jax.ShapeDtypeStruct(shape, BF16)
    hbm = pl.BlockSpec(memory_space=pl.ANY)
    vmem = pl.BlockSpec(memory_space=pltpu.VMEM)
    wide = 2 * QW + 2 * HD
    dq, dkvr, zr = pl.pallas_call(
        kernel,
        out_shape=(out(TOK, 8 * REP * HD), out(2, 8, 2, TOK, HD), out(2, 9, 64, HD)),
        in_specs=[hbm] * 8,
        out_specs=(hbm,) * 3,
        scratch_shapes=[
            pltpu.SMEM((2,), jnp.int32),
            pltpu.SMEM((2,), jnp.int32),
            pltpu.VMEM((8, 128), jnp.int32),
            pltpu.VMEM((2, 8, 128), jnp.int32),
            pltpu.SMEM((2, 8, 128), jnp.int32),
            vm(TOK, 8 * QW),
            vm(TOK, 8 * QW),
            vm(TOK, 8 * HD),
            vm(TOK, 8 * HD),
            vm(8, TOK, wide),
            vm(2, 2, 4, TOK, HD),
            vm(8, TOK, wide),
            vm(2, 8, TOK, HD),
            vm(8, 4, 2, 64, HD),
            vm(8, 4, 2, 64, HD),
            vm(2, 4, 2, 4, 64, HD),
            vm(2, 8, 2, 4, 64, HD),
            vm(8, TOK, REP * HD),
            vm(2, 8, 2, TOK, HD),
            vm(2, 2, 2, 2, TOK, HD),
            vm(2, 4, 2, 64, HD),
            vm(2, 4, 2, 64, HD),
            vm(2, 4, 2, 64, HD),
            vm(2, 4, 2, 64, HD),
            vm(2, 4, 2, 64, HD),
            vm(2, 4, 2, 64, HD),
            vm(2, 8, 2, 64, HD),
            vm(2, 4, 2, 64, HD),
            vm(8, ROWS, HD),
            vm(8, ROWS, HD),
            vm(4, PLEN + RCAP, HD),
            vm(PLEN + RCAP, HD),
            pltpu.VMEM((2, PLEN + RCAP, ROWS), F32),
            pltpu.VMEM((2, PLEN + RCAP, ROWS), F32),
            pltpu.VMEM((8, PLEN + RCAP, ROWS), F32),
            vm(2, PLEN + RCAP, ROWS),
            vm(8, PLEN + RCAP, ROWS),
            dma((4,)),
            dma((4,)), dma((8,)), dma((8,)), dma((2, 2)), dma((2, 2)), dma((2, 8)), dma((2, 8)),
            pltpu.SemaphoreType.REGULAR((2,)), pltpu.SemaphoreType.REGULAR((2,)),
            dma((2, 5)), dma((2, 8, 2)),
            dma((2, 2, 3, 8)), dma((2, 8)), dma((2, 2, 8)), dma((2, 2, 8)), dma((2, 2, 8)), dma((2, 2, 8)),
            dma((8,)), dma((8,)), dma((8,)), dma((16,)), dma((2, 2, 2)), dma((2, 2, 2)), dma((2, 2, 4)), dma((2, 8)),
            dma((2, 4, 4)), dma((2, 4, 4)), dma((2, 2, 4)), dma((2, 2, 4)),
            dma((2, 2, 8)), dma((2, 9)), dma((2, 4)),
        ],
        compiler_params=pltpu.CompilerParams(
            collective_id=0, has_side_effects=True, vmem_limit_bytes=62 * 1024 * 1024
        ),
        cost_estimate=pl.CostEstimate(flops=2_000_000_000, bytes_accessed=4_000_000, transcendentals=1_400_000),
    )(queries, keys, values, out_grad, prefix_keys, prefix_values, lengths, prompt_of)
    return pl.pallas_call(
        finish,
        out_shape=(
            jax.ShapeDtypeStruct(queries.shape, BF16),
            jax.ShapeDtypeStruct(keys.shape, BF16),
            jax.ShapeDtypeStruct(values.shape, BF16),
            jax.ShapeDtypeStruct(prefix_keys.shape, BF16),
            jax.ShapeDtypeStruct(prefix_values.shape, BF16),
        ),
        in_specs=[hbm] * 3,
        out_specs=(hbm,) + (vmem,) * 4,
        scratch_shapes=[vm(TOK, 8 * REP * HD), vm(2, 8, 2, TOK, HD), vm(2, 9, 64, HD), dma((4,))],
        compiler_params=pltpu.CompilerParams(vmem_limit_bytes=62 * 1024 * 1024),
        name="finish",
    )(dq, dkvr, zr)


def solution(mesh):
    in_specs = (
        P(("resp", "tp"), None),
        P(("resp", "tp"), None),
        P(("resp", "tp"), None),
        P(("resp", "tp"), None),
        P("resp", "tp"),
        P("resp", "tp"),
        P("resp"),
        P("resp"),
    )
    out_specs = (
        P(("resp", "tp"), None),
        P(("resp", "tp"), None),
        P(("resp", "tp"), None),
        P("resp", "tp"),
        P("resp", "tp"),
    )
    return jax.shard_map(body, mesh=mesh, in_specs=in_specs, out_specs=out_specs, check_vma=False)
```

```python
import functools
import math

import jax
import jax.numpy as jnp
from jax import lax
from jax.experimental import pallas as pl
from jax.experimental.pallas import tpu as pltpu
from jax.sharding import PartitionSpec as P

HD = 128
RCAP = 128
PLEN = 512
PROMPTS = 8
X, Y, ZL, C, ZH = 4, 4, 8, 2, 2
Z = ZL * ZH
REP = 8
QW = REP * HD
LATE = 6
TOK = 32
MESH = pl.DeviceIdType.MESH
F32 = jnp.float32
BF16 = jnp.bfloat16
SCALE = 1.0 / math.sqrt(HD)
SCALE2 = SCALE * math.log2(math.e)


def where_is(x, y, z, c):
    return {"resp": x * (ZL * C) + lax.rem(z, ZL) * C + c, "tp": y * ZH + z // ZL}


def remote(src, dst, send, recv, device):
    return pltpu.make_async_remote_copy(
        src_ref=src, dst_ref=dst, send_sem=send, recv_sem=recv, device_id=device, device_id_type=MESH
    )


def dot_nt(a, b):
    return lax.dot_general(a, b, (((1,), (1,)), ((), ())), preferred_element_type=F32)


def dot_nn(a, b):
    return lax.dot_general(a, b, (((1,), (0,)), ((), ())), preferred_element_type=F32)


def dot_tn(a, b):
    return lax.dot_general(a, b, (((0,), (0,)), ((), ())), preferred_element_type=F32)


ROWS = REP * TOK
CHUNK = 128
CHUNKS = (PLEN + RCAP) // CHUNK


def kernel(
    q_in, k_in, v_in, g_in, pk_in, pv_in, len_in, prompt_in,
    dq_out, dkvr, zr,
    len_s, prompt_s, aux_l, aux_v, aux_s, qs, gs, ks, vs, side, kvrel, rows, kvx, pkb, pvb,
    term, dense, dqs, dkvs, dkrel,
    ra, rb, ra1, rb1, ra2, rb2, xsum, zrel, qh, gh, kk, vv, s_scr, dp_scr, p_scr, b_scr, ds_scr,
    aux_sem, in_sem, r_ss, r_rs, kr_ss, kr_rs, kx_ss, kx_rs,
    near_in, far_in, p_ss, p_rs, z_ss, z_rs, x_ss, x_rs, x2_ss, x2_rs,
    dq_ss, dq_rs, dkv_ss, dkv_rs, dr_ss, dr_rs, df_ss, df_rs,
    rx_ss, rx_rs, rx2_ss, rx2_rs, rz_ss, rz_rs, rl_rs,
):
    r = lax.axis_index("resp")
    t = lax.axis_index("tp")
    x, zl, c = r // (ZL * C), lax.rem(r // C, ZL), lax.rem(r, C)
    y, zh = t // ZH, lax.rem(t, ZH)
    z = zh * ZL + zl
    head = y * C + c
    xr, xl = lax.rem(x + 1, X), lax.rem(x + X - 1, X)
    xo = lax.rem(x + 2, X)
    zr_, zl_ = lax.rem(z + 1, Z), lax.rem(z + Z - 1, Z)
    here = where_is(x, y, z, c)

    z4 = (lax.rem(z + 4, Z), lax.rem(z + Z - 4, Z))
    y_odd = lax.rem(y, 2) == 1

    loads = [
        pltpu.make_async_copy(k_in, ks, in_sem.at[0]),
        pltpu.make_async_copy(v_in, vs, in_sem.at[1]),
        pltpu.make_async_copy(q_in, qs, in_sem.at[2]),
        pltpu.make_async_copy(g_in, gs, in_sem.at[3]),
    ]
    for cp in loads:
        cp.start()
    ints = [
        pltpu.make_async_copy(len_in, len_s, aux_sem.at[0]),
        pltpu.make_async_copy(prompt_in, prompt_s, aux_sem.at[3]),
    ]
    for cp in ints:
        cp.start()

    barrier = pltpu.get_barrier_semaphore()

    def greet(x_, y_, z_, c_):
        pl.semaphore_signal(barrier, inc=1, device_id=where_is(x_, y_, z_, c_), device_id_type=MESH)

    def greet_y(i, carry):
        y_ = lax.rem(y + i, Y)
        greet(x, y_, z, c)
        greet(x, y_, z, 1 - c)
        return carry

    lax.fori_loop(1, Y, greet_y, 0)
    greet(xr, y, z, c)
    greet(xl, y, z, c)
    greet(xo, y, z, c)
    greet(x, y, z, 1 - c)
    z2 = (lax.rem(z + 2, Z), lax.rem(z + Z - 2, Z))
    for z_ in (zr_, zl_) + z2:
        greet(x, y, z_, c)
        greet(x, y, z_, 1 - c)

    def tell(sem):
        for i in (0, 1):
            pl.semaphore_signal(sem.at[i], inc=1, device_id=where_is(x, y, z2[i], c), device_id_type=MESH)

    def told(sem):
        for i in (0, 1):
            pl.semaphore_wait(sem.at[i], 1)

    for cp in loads:
        cp.wait()
    for h in range(8):
        side[h, :, :QW] = qs[:, h * QW : (h + 1) * QW]
        side[h, :, QW : 2 * QW] = gs[:, h * QW : (h + 1) * QW]
        side[h, :, 2 * QW : 2 * QW + HD] = ks[:, h * HD : (h + 1) * HD]
        side[h, :, 2 * QW + HD :] = vs[:, h * HD : (h + 1) * HD]

    pl.semaphore_wait(barrier, 2 * (Y - 1) + 3 + 1 + 8)
    tell(near_in)

    def chunk(w, x_, zl_src):
        return prefix[w].at[x_ * 2 + zl_src // 4, lax.rem(zl_src, 4)]

    own_core = c == zh
    prefix_in = (pk_in, pv_in)
    prefix = (pkb, pvb)

    def mine_near(w):
        return pltpu.make_async_copy(prefix_in[w], chunk(w, x, zl).at[c], p_ss.at[w, 0])

    def mine_far(w, i):
        z_ = (z, zr_, z2[0], zl_, z2[1])[i]
        ref = chunk(w, x, zl).at[c]
        return remote(prefix_in[w], ref, p_ss.at[w, i], p_rs.at[w, zl, c], where_is(x, y, z_, zh))

    def mine_send(w):
        for i in (2, 4, 1, 3):
            mine_far(w, i).start()

        @pl.when(own_core)
        def _():
            mine_near(w).start()

        @pl.when(jnp.logical_not(own_core))
        def _():
            mine_far(w, 0).start()

    def halves_wait(w, s):
        for half in (0, 1):
            ref = chunk(w, x, s).at[half]
            remote(prefix_in[w], ref, p_ss.at[w, 0], p_rs.at[w, s, half], here).wait_recv()

    def mine_wait(w):
        @pl.when(own_core)
        def _():
            mine_near(w).wait()
            remote(prefix_in[w], chunk(w, x, zl).at[1 - c], p_ss.at[w, 0], p_rs.at[w, zl, 1 - c], here).wait_recv()

    mine_send(0)
    mine_send(1)

    def slot_of(y_, c_):
        return ((y_ // 2) * 2 + c_) * 2 + lax.rem(y_, 2)

    my_slot = slot_of(y, c)

    def row_copy(dy, dc):
        y_, c_ = lax.rem(y + dy, Y), lax.rem(c + dc, C)
        return remote(
            side.at[y_ * C + c_], rows.at[my_slot], r_ss.at[dy * 2 + dc], r_rs.at[my_slot], where_is(x, y_, z, c_)
        )

    def unseen(zh_src, odd):
        return jnp.logical_and(zh_src == 1, odd)

    def rel_copy(kv, way):
        src = side.at[pl.ds(4 * way, 4), :, pl.ds(2 * QW + kv * HD, HD)]
        return remote(src, kvrel.at[kv, way], kr_ss.at[kv, way], kr_rs.at[kv, way], where_is(x, y, z4[way], c))

    def rel_src(way):
        return z4[1 - way] // ZL

    def rel_on(kv, way):
        return [
            remote(
                kvrel.at[kv, way, i],
                kvx.at[kv, my_slot],
                kx_ss.at[kv, way * 4 + i],
                kx_rs.at[kv, my_slot],
                where_is(x, 2 * way + i // 2, z4[way], i % 2),
            )
            for i in range(4)
        ]

    def rel_start(kv):
        @pl.when(jnp.logical_not(unseen(zh, y_odd)))
        def _():
            for way in (0, 1):
                rel_copy(kv, way).start()

    def rel_pass(kv):
        for way in (0, 1):

            @pl.when(jnp.logical_not(unseen(rel_src(way), y_odd)))
            def _():
                rel_copy(kv, way).wait_recv()
                for cp in rel_on(kv, way):
                    cp.start()

    def kvx_wait(kv):
        for y_ in range(Y):
            for c_ in range(C):

                @pl.when(jnp.logical_not(unseen(1 - zh, y_ % 2 == 1)))
                def _():
                    ref = kvx.at[kv, slot_of(y_, c_)]
                    remote(ref, ref, kx_ss.at[kv, 0], kx_rs.at[kv, slot_of(y_, c_)], here).wait_recv()

    far = [(dy, dc) for dc in (0, 1) for dy in (1, 3, 2, 0) if (dy, dc) != (0, 0)]

    def y_start(*pairs):
        for dy, dc in pairs:
            row_copy(dy, dc).start()

    y_start((2, 0))
    own = pltpu.make_async_copy(side.at[head], rows.at[my_slot], r_ss.at[0])
    own.start()

    for cp in ints:
        cp.wait()
    lane = lax.broadcasted_iota(jnp.int32, (8, 128), 1)
    aux_l[...] = jnp.where(
        lane == 0,
        prompt_s[0],
        jnp.where(lane == 1, prompt_s[1], jnp.where(lane == 2, len_s[0], len_s[1])),
    )
    aux_own = pltpu.make_async_copy(aux_l, aux_v.at[c], aux_sem.at[0])
    aux_own.start()
    aux_far = remote(aux_l, aux_v.at[c], aux_sem.at[1], aux_sem.at[2], where_is(x, y, z, 1 - c))
    aux_far.start()

    def z_copy(w, way, far_, s):
        up_dev = where_is(x, y, lax.rem(z + 1 + far_, Z), c)
        down_dev = where_is(x, y, lax.rem(z + Z - 1 - far_, Z), c)
        ref = chunk(w, x, s)
        return remote(ref, ref, z_ss.at[w, way, far_, s], z_rs.at[w, s], up_dev if way == 0 else down_dev)

    def x_copy(w, way, s):
        ref, dev = chunk(w, x, s), where_is(xr if way == 0 else xl, y, z, c)
        return remote(ref, ref, x_ss.at[w, way, s], x_rs.at[w, way, s], dev)

    def x_arrived(w, way, s):
        ref = chunk(w, xl if way == 0 else xr, s)
        return remote(ref, ref, x_ss.at[w, way, s], x_rs.at[w, way, s], here)

    def x2_copy(w, way, s):
        ref, dev = chunk(w, xl if way == 0 else xr, s).at[way], where_is(xr if way == 0 else xl, y, z, c)
        return remote(ref, ref, x2_ss.at[w, way, s], x2_rs.at[w, way, s], dev)

    def x3_copy(w, s):
        ref = chunk(w, x, s)
        return remote(ref, ref, x2_ss.at[w, 0, s], x2_rs.at[w, 0, s], where_is(xo, y, z, c))

    def x3_arrived(w, s):
        ref = chunk(w, xo, s)
        return remote(ref, ref, x2_ss.at[w, 0, s], x2_rs.at[w, 0, s], here)

    def x2_arrived(w, way, s):
        ref = chunk(w, xo, s).at[way]
        return remote(ref, ref, x2_ss.at[w, way, s], x2_rs.at[w, way, s], here)

    def source(way, k):
        s = lax.rem(z + (Z - k if way == 0 else k), Z)
        return s // ZL == c, lax.rem(s, ZL)

    def x_start(w, s):
        x_copy(w, 0, s).start()
        x_copy(w, 1, s).start()

    def forwards(w, way, j, s):
        return [z_copy(w, way, i, s) for i in (2, 1, 0) if not (j == 2 and way == 1 and i == 2)]

    def stop(w, j):
        for way in (0, 1):
            live, s = source(way, 3 * j - 1 if j else 0)

            @pl.when(live)
            def _():
                if j == 1:
                    halves_wait(w, s)
                elif j == 2:
                    z_copy(w, way, 0, s).wait_recv()
                if j > 0:
                    for cp in forwards(w, way, j, s):
                        cp.start()

        for way in (0, 1):
            live, s = source(way, 3 * j - 1 if j else 0)

            @pl.when(live)
            def _():
                if j > 0 or way == 0:
                    x_start(w, s)

        for k in ((), (1,), (3, 4))[j]:
            for way in (0, 1):
                arrive(w, way, k)

    def arrive(w, way, k):
        live, s = source(way, k)

        @pl.when(live)
        def _():
            if k == 1:
                halves_wait(w, s)
            else:
                z_copy(w, way, 0, s).wait_recv()
            x_start(w, s)
            if k >= LATE:
                x3_copy(w, s).start()

    def stop_sent(w, j):
        for way in (0, 1):
            live, s = source(way, 3 * j - 1)

            @pl.when(live)
            def _():
                for cp in forwards(w, way, j, s):
                    cp.wait_send()

    def last_arrivals(w):
        for way, k in ((0, 6), (1, 6), (0, 7), (1, 7), (0, 8)):
            arrive(w, way, k)

    def pass_on(w, way, k):
        live, s = source(way, k)

        @pl.when(live)
        def _():
            for x_way in (0, 1):
                x_arrived(w, x_way, s).wait_recv()
                x2_copy(w, x_way, s).start()

    def all_on(w, low, high):
        for k in range(low, high):
            pass_on(w, 0, k)
            if 0 < k < 8:
                pass_on(w, 1, k)

    all_sources = [(way, k) for k in range(9) for way in (0, 1) if way == 0 or 0 < k < 8]

    def x2_wait(w):
        for way, k in all_sources:
            live, s = source(way, k)

            @pl.when(live)
            def _():
                if k >= LATE:
                    x_arrived(w, 0, s).wait_recv()
                    x_arrived(w, 1, s).wait_recv()
                    x3_arrived(w, s).wait_recv()
                else:
                    x2_arrived(w, 0, s).wait_recv()
                    x2_arrived(w, 1, s).wait_recv()

    mine_wait(0)
    stop(0, 0)
    y_start((1, 0))
    mine_wait(1)
    told(near_in)
    tell(far_in)
    stop(0, 1)
    stop(1, 0)
    told(far_in)
    rel_start(0)
    y_start((2, 1), (3, 0))
    stop(0, 2)
    stop(1, 1)
    rel_pass(0)
    rel_start(1)
    y_start((1, 1), (3, 1))
    last_arrivals(0)
    y_start((0, 1))
    stop(1, 2)
    rel_pass(1)
    all_on(0, 0, LATE)
    last_arrivals(1)

    for dy, dc in far:
        ref = rows.at[slot_of(lax.rem(y + dy, Y), lax.rem(c + dc, C))]
        remote(ref, ref, r_ss.at[0], r_rs.at[slot_of(lax.rem(y + dy, Y), lax.rem(c + dc, C))], here).wait_recv()
    kvx_wait(0)
    own.wait()
    aux_own.wait()
    remote(aux_l, aux_v.at[1 - c], aux_sem.at[1], aux_sem.at[2], here).wait_recv()

    to_smem = pltpu.make_async_copy(aux_v, aux_s, aux_sem.at[3])
    to_smem.start()
    to_smem.wait()

    x2_wait(0)

    def q_cols(ref, h):
        return ref.at[:, pl.ds(pl.multiple_of(h * QW, QW), QW)]

    def dq_copy(sl):
        rho = sl // 2
        y_, c_ = (rho // 2) * 2 + lax.rem(sl, 2), lax.rem(rho, 2)
        dst = q_cols(dq_out, head)
        return (
            sl == my_slot,
            remote(dqs.at[sl], dst, dq_ss.at[sl], dq_rs.at[head], where_is(x, y_, z, c_)),
            pltpu.make_async_copy(dqs.at[sl], dst, dq_ss.at[sl]),
        )

    def dkv_copy(rho, yb):
        y_, c_ = (rho // 2) * 2 + yb, lax.rem(rho, 2)
        i = dk_slot(rho, yb)
        src, dst = dkvs.at[zh, i], dkvr.at[zh, head]
        return (
            jnp.logical_and(y_ == y, c_ == c),
            remote(src, dst, dkv_ss.at[i], dkv_rs.at[zh * 8 + head], where_is(x, y_, z, c_)),
            pltpu.make_async_copy(src, dst, dkv_ss.at[i]),
        )

    def dk_slot(rho, yb):
        return (rho // 2) * 4 + yb * 2 + lax.rem(rho, 2)

    def drel_copy(kv, way, yb):
        dev = where_is(x, y, jnp.where(way == 0, z4[0], z4[1]), c)
        src = dkvs.at[1 - zh, pl.ds(way * 4 + yb * 2, 2), kv]
        return remote(src, dkrel.at[kv, way, yb], dr_ss.at[kv, way, yb], dr_rs.at[kv, way, yb], dev)

    def drel_start(kv, way):
        drel_copy(kv, way, 0).start()

        @pl.when(zh == 1)
        def _():
            drel_copy(kv, way, 1).start()

    def drel_on(kv, way, yb):
        zs = rel_src(way)
        return [
            remote(
                dkrel.at[kv, way, yb, i],
                dkvr.at[zs, head, kv],
                df_ss.at[kv, way, yb * 2 + i],
                df_rs.at[kv, head],
                where_is(x, 2 * way + yb, z4[way], i),
            )
            for i in (0, 1)
        ]

    def drel_pass(kv, way):
        drel_copy(kv, way, 0).wait_recv()
        for cp in drel_on(kv, way, 0):
            cp.start()

        @pl.when(rel_src(way) == 1)
        def _():
            drel_copy(kv, way, 1).wait_recv()
            for cp in drel_on(kv, way, 1):
                cp.start()

    def send(copies):
        local, far_cp, near_cp = copies

        @pl.when(local)
        def _():
            near_cp.start()

        @pl.when(jnp.logical_not(local))
        def _():
            far_cp.start()

    def sent(copies):
        local, far_cp, near_cp = copies

        @pl.when(local)
        def _():
            near_cp.wait()

        @pl.when(jnp.logical_not(local))
        def _():
            far_cp.wait_send()

    def fold(a, op):
        return op(a.reshape(CHUNK // 8, 8, ROWS), 0)

    def keys_of(kv, prompt, rho, to):
        to[:PLEN] = prefix[kv][prompt].reshape(PLEN, HD)
        for b in (0, 1):
            i = rho * 2 + b
            near = pl.ds(pl.multiple_of(PLEN + (2 * b + zh) * TOK, TOK), TOK)
            over = pl.ds(pl.multiple_of(PLEN + (2 * b + 1 - zh) * TOK, TOK), TOK)
            low = 2 * QW + kv * HD
            to[near] = rows[i, :, low : low + HD]
            crossed = kvx[kv, i].astype(F32)
            if b == 1:
                crossed = jnp.where(zh == 1, crossed, 0.0)
            to[over] = crossed.astype(BF16)

    def leave(kv, rho, grad):
        for i in range(4):
            for ct in (0, 1):
                low = (i * 2 + ct) * 64
                term[kv, rho, ct, i] = grad[low : low + 64].astype(BF16)
        for tb in range(4):
            low = PLEN + tb * TOK
            dkvs[tb % 2, dk_slot(rho, tb // 2), kv] = grad[low : low + TOK].astype(BF16)

    def weigh(rho, carry):
        prompt = aux_s[lax.rem(rho, 2), 0, rho // 2]
        length = aux_s[lax.rem(rho, 2), 0, 2 + rho // 2]
        k_rho = kk.at[rho]
        keys_of(0, prompt, rho, k_rho)
        acc = []
        for b in (0, 1):
            i = rho * 2 + b
            qa, ga = rows[i, :, :QW], rows[i, :, QW : 2 * QW]
            tok = lax.broadcasted_iota(jnp.int32, (TOK, HD), 0) + (64 * b + TOK * zh)
            keep = jnp.where(tok < length, 1.0, 0.0)
            q = jnp.concatenate([qa[:, h * HD : (h + 1) * HD] for h in range(REP)], axis=0)
            g = jnp.concatenate(
                [(ga[:, h * HD : (h + 1) * HD].astype(F32) * keep).astype(BF16) for h in range(REP)], axis=0
            )
            qh[i] = q
            gh[i] = g
            top = jnp.full((8, ROWS), -jnp.inf, F32)
            for n in range(CHUNKS):
                at = slice(n * CHUNK, (n + 1) * CHUNK)
                s = dot_nt(k_rho[at], q)
                if n == CHUNKS - 1:
                    col = lax.broadcasted_iota(jnp.int32, (CHUNK, ROWS), 1)
                    key = lax.broadcasted_iota(jnp.int32, (CHUNK, ROWS), 0)
                    s = jnp.where(key <= lax.rem(col, TOK) + (64 * b + TOK * zh), s, -jnp.inf)
                s_scr[b, at] = s
                top = jnp.maximum(top, fold(s, jnp.max))
            top = jnp.max(top, 0, keepdims=True)
            total = jnp.zeros((8, ROWS), F32)
            for n in range(CHUNKS):
                at = slice(n * CHUNK, (n + 1) * CHUNK)
                e = jnp.exp2((s_scr[b, at] - top) * SCALE2)
                s_scr[b, at] = e
                total = total + fold(e, jnp.sum)
            inv = 1.0 / jnp.sum(total, 0, keepdims=True)
            for n in range(CHUNKS):
                at = slice(n * CHUNK, (n + 1) * CHUNK)
                p = s_scr[b, at] * inv
                p_scr[i, at] = p
                b_scr[b, at] = p.astype(BF16)
            acc.append(dot_nn(b_scr[b], g))
        leave(1, rho, acc[0] + acc[1])

        @pl.when(lax.rem(rho, 2) == 1)
        def _():
            drel_start(1, rho // 2)

        @pl.when(rho == 0)
        def _():
            all_on(1, 0, 3)

        @pl.when(rho == 1)
        def _():
            all_on(1, 3, LATE)

        return carry

    def differentiate(rho, carry):
        prompt = aux_s[lax.rem(rho, 2), 0, rho // 2]
        keys_of(1, prompt, rho, vv)
        acc = []
        for b in (0, 1):
            i = rho * 2 + b
            mixed = jnp.zeros((8, ROWS), F32)
            for n in range(CHUNKS):
                at = slice(n * CHUNK, (n + 1) * CHUNK)
                dp = dot_nt(vv[at], gh[i])
                dp_scr[b, at] = dp
                mixed = mixed + fold(p_scr[i, at] * dp, jnp.sum)
            delta = jnp.sum(mixed, 0, keepdims=True)
            for n in range(CHUNKS):
                at = slice(n * CHUNK, (n + 1) * CHUNK)
                ds_scr[i, at] = (p_scr[i, at] * (dp_scr[b, at] - delta)).astype(BF16)
            acc.append(dot_nn(ds_scr[i], qh[i]))
        leave(0, rho, (acc[0] + acc[1]) * SCALE)

        @pl.when(lax.rem(rho, 2) == 1)
        def _():
            drel_start(0, rho // 2)

        for b in (0, 1):
            send(dkv_copy(rho, b))

        @pl.when(rho == 2)
        def _():
            for way in (0, 1):
                drel_pass(1, way)

        first(1, order(rho))

        @pl.when(rho >= 2)
        def _():
            second(1, order(rho - 2))

        return carry

    def query_grads(rho, carry):
        for b in (0, 1):
            i = rho * 2 + b
            dq = (dot_tn(kk[rho], ds_scr[i]) * SCALE).T.astype(BF16)
            for h in range(REP):
                dqs[i, :, h * HD : (h + 1) * HD] = dq[h * TOK : (h + 1) * TOK]
        return carry

    def part(w, x_, n, half):
        return dense.at[w, x_ * 2 + n // 2, half, pl.ds(lax.rem(n, 2) * 2, 2)]

    def own_part(w, x_, n, half):
        return dense[w, x_ * 2 + n // 2, half, pl.ds(lax.rem(n, 2) * 2, 2)].astype(F32)

    def rx_copy(w, way, n):
        if way == 0:
            src, dst, dev = part(w, xo, n, 0), ra.at[w, n], where_is(xr, y, z, c)
        elif way == 1:
            src, dst, dev = part(w, xo, n, 1), rb.at[w, n], where_is(xl, y, z, c)
        elif way == 2:
            src, dst, dev = part(w, xr, n, 1), rb1.at[w, n], where_is(xr, y, z, c)
        else:
            src, dst, dev = part(w, xl, n, 0), ra1.at[w, n], where_is(xl, y, z, c)
        return remote(src, dst, rx_ss.at[w, way, n], rx_rs.at[w, way, n], dev)

    def rx2_copy(w, way, n):
        if way == 0:
            src, dst, dev = ra.at[w, n], ra2.at[w, n], where_is(xr, y, z, c)
        else:
            src, dst, dev = rb.at[w, n], rb2.at[w, n], where_is(xl, y, z, c)
        return remote(src, dst, rx2_ss.at[w, way, n], rx2_rs.at[w, way, n], dev)

    rising = (zh != c) == (zl < 4)

    def order(i):
        n = lax.rem(i, 2) * 2 + i // 2
        return jnp.where(rising, n, 3 - n)

    def spread_all(w):
        def spread_half(i, carry):
            ip = jnp.where(rising, i, 1 - i)
            two = pl.ds(ip * 2, 2)

            def spread(p, carry):
                acc = jnp.zeros((2, 2, 64, HD), F32)
                for rho in range(4):
                    hit = aux_s[rho % 2, 0, rho // 2] == p
                    acc = acc + jnp.where(hit, term[w, rho, :, two].astype(F32), 0.0)
                dense[w, p, :, two] = acc.astype(BF16)
                return carry

            lax.fori_loop(0, PROMPTS, spread, 0)
            for j in (0, 1):
                for way in (0, 1):
                    rx_copy(w, way, order(2 * i + j)).start()
            return carry

        lax.fori_loop(0, 2, spread_half, 0)

    def z_dist(zt):
        return lax.rem(c * ZL + zt - z + 23, Z) - 7

    def z_direct(w, zt, ct, d):
        src, dst, zd = xsum.at[w, zt, ct], zr.at[w, d + 4], c * ZL + zt
        return (
            jnp.logical_and(d == 0, ct == c),
            remote(src, dst, rz_ss.at[w, ct, zt], rz_rs.at[w, d + 4], where_is(x, y, zd, ct)),
            pltpu.make_async_copy(src, dst, rz_ss.at[w, ct, zt]),
        )

    def z_stop(w, zt, d):
        up_ = d > 0
        zd = lax.rem(z + Z + jnp.where(up_, d - 4, d + 4), Z)
        i = jnp.where(up_, d, -d) - 5
        return remote(xsum.at[w, zt], zrel.at[w, i], rz_ss.at[w, 0, zt], rl_rs.at[w, i], where_is(x, y, zd, c))

    def is_far(d):
        return jnp.logical_or(d > 4, d < -4)

    def is_near(d):
        return jnp.logical_and(d < 4, d > -4)

    def first(w, n):
        rx_copy(w, 0, n).wait_recv()
        ra[w, n] = (ra[w, n].astype(F32) + own_part(w, xr, n, 0)).astype(BF16)
        rx2_copy(w, 0, n).start()
        rx_copy(w, 2, n).start()
        rx_copy(w, 1, n).wait_recv()
        rb[w, n] = (rb[w, n].astype(F32) + own_part(w, xl, n, 1)).astype(BF16)
        rx2_copy(w, 1, n).start()
        rx_copy(w, 3, n).start()

    def second(w, n):
        rx_copy(w, 3, n).wait_recv()
        rx2_copy(w, 0, n).wait_recv()
        one = own_part(w, x, n, 0) + ra1[w, n].astype(F32) + ra2[w, n].astype(F32)
        rx_copy(w, 2, n).wait_recv()
        rx2_copy(w, 1, n).wait_recv()
        two = own_part(w, x, n, 1) + rb1[w, n].astype(F32) + rb2[w, n].astype(F32)
        for i in (0, 1):
            zt = 2 * n + i
            xsum[w, zt, 0] = one[i].astype(BF16)
            xsum[w, zt, 1] = two[i].astype(BF16)
            d = z_dist(zt)

            @pl.when(is_near(d))
            def _():
                for ct in (0, 1):
                    send(z_direct(w, zt, ct, d))

            @pl.when(is_far(d))
            def _():
                z_stop(w, zt, d).start()

    zt_stop = lax.rem(zl + 4, ZL)
    d_stop = z_dist(zt_stop)

    def stop_sum(w):
        def stop_wait(i, carry):
            @pl.when(jnp.logical_or(i < 3, d_stop > 0))
            def _():
                remote(zrel.at[w, i], zrel.at[w, i], rz_ss.at[w, 0, 0], rl_rs.at[w, i], here).wait_recv()

            return carry

        lax.fori_loop(0, 4, stop_wait, 0)
        for ct in (0, 1):
            three = xsum[w, zt_stop, ct].astype(F32)
            for i in range(3):
                three = three + zrel[w, i, ct].astype(F32)

            @pl.when(d_stop > 0)
            def _():
                xsum[w, zt_stop, ct] = (three + zrel[w, 3, ct].astype(F32)).astype(BF16)

            @pl.when(d_stop < 0)
            def _():
                xsum[w, zt_stop, ct] = three.astype(BF16)

            z_direct(w, zt_stop, ct, d_stop)[1].start()

    lax.fori_loop(0, 4, weigh, 0)
    spread_all(1)
    x2_wait(1)
    kvx_wait(1)
    lax.fori_loop(0, 4, differentiate, 0)
    spread_all(0)
    drel_pass(0, 0)
    lax.fori_loop(0, 4, query_grads, 0)
    second(1, order(2))
    second(1, order(3))

    def last(i, carry):
        @pl.when(i < 4)
        def _():
            first(0, order(i))

        @pl.when(i == 1)
        def _():
            drel_pass(0, 1)

        @pl.when(i == 2)
        def _():
            stop_sum(1)

        @pl.when(i >= 1)
        def _():
            second(0, order(i - 1))
            send(dq_copy(2 * i - 2))
            send(dq_copy(2 * i - 1))

        return carry

    lax.fori_loop(0, 5, last, 0)
    stop_sum(0)

    def dkv_wait(h, carry):
        near = dkvr.at[zh, h]

        @pl.when(h != head)
        def _():
            remote(near, near, dkv_ss.at[0], dkv_rs.at[zh * 8 + h], here).wait_recv()

        @pl.when(jnp.logical_not(unseen(zh, y_odd)))
        def _():
            for kv in (0, 1):
                over = dkvr.at[1 - zh, h, kv]
                remote(over, over, dkv_ss.at[0], df_rs.at[kv, h], here).wait_recv()

        return carry

    def dkv_sent(i, carry):
        for yb in (0, 1):
            sent(dkv_copy(i, yb))
        return carry

    lax.fori_loop(0, 4, dkv_sent, 0)
    lax.fori_loop(0, 8, dkv_wait, 0)
    def z_sent(i, carry):
        w, n = i // ZL, lax.rem(i, ZL)
        d = z_dist(n)

        @pl.when(is_far(d))
        def _():
            z_stop(w, n, d).wait_send()

        @pl.when(jnp.logical_not(is_far(d)))
        def _():
            for ct in (0, 1):
                sent(z_direct(w, n, ct, d))

        return carry

    def z_wait(i, carry):
        for w in (0, 1):

            @pl.when(jnp.logical_not(jnp.logical_and(own_core, i == 4)))
            def _():
                remote(zr.at[w, i], zr.at[w, i], rz_ss.at[w, 0, 0], rz_rs.at[w, i], here).wait_recv()

        return carry

    lax.fori_loop(0, 2 * ZL, z_sent, 0)
    lax.fori_loop(0, 9, z_wait, 0)

    def dq_wait(h, carry):
        @pl.when(h != head)
        def _():
            ref = q_cols(dq_out, h)
            remote(ref, ref, dq_ss.at[0], dq_rs.at[h], here).wait_recv()

        return carry

    def dq_sent(i, carry):
        sent(dq_copy(i))
        return carry

    lax.fori_loop(0, 8, dq_sent, 0)
    lax.fori_loop(0, 8, dq_wait, 0)
    aux_far.wait_send()
    for dy, dc in far:
        row_copy(dy, dc).wait_send()

    @pl.when(jnp.logical_not(unseen(zh, y_odd)))
    def _():
        for kv in (0, 1):
            for way in (0, 1):
                rel_copy(kv, way).wait_send()

    for way in (0, 1):

        @pl.when(jnp.logical_not(unseen(rel_src(way), y_odd)))
        def _():
            for cp in rel_on(0, way) + rel_on(1, way):
                cp.wait_send()

        for kv in (0, 1):
            drel_copy(kv, way, 0).wait_send()
            for cp in drel_on(kv, way, 0):
                cp.wait_send()

        @pl.when(zh == 1)
        def _():
            for kv in (0, 1):
                drel_copy(kv, way, 1).wait_send()

        @pl.when(rel_src(way) == 1)
        def _():
            for kv in (0, 1):
                for cp in drel_on(kv, way, 1):
                    cp.wait_send()

    for w in (0, 1):
        for i in (1, 2, 3, 4):
            mine_far(w, i).wait_send()

        @pl.when(jnp.logical_not(own_core))
        def _():
            mine_far(w, 0).wait_send()

    for w in (0, 1):
        for j in (1, 2):
            stop_sent(w, j)

    def x_sent(s, carry):
        for w in (0, 1):
            for way in (0, 1):
                x_copy(w, way, s).wait_send()
        return carry

    lax.fori_loop(0, ZL, x_sent, 0)
    for w in (0, 1):
        for way, k in all_sources:
            live, s = source(way, k)

            @pl.when(live)
            def _():
                if k >= LATE:
                    x3_copy(w, s).wait_send()
                else:
                    x2_copy(w, 0, s).wait_send()
                    x2_copy(w, 1, s).wait_send()

    def rx_sent(n, carry):
        for w in (0, 1):
            for way in range(4):
                rx_copy(w, way, n).wait_send()
            for way in (0, 1):
                rx2_copy(w, way, n).wait_send()
        return carry

    lax.fori_loop(0, 4, rx_sent, 0)


def finish(dq_in, dkvr_in, zr_in, dq_out, dk_out, dv_out, gpk_out, gpv_out, dq, dkvr, zr, sem):
    loads = [
        pltpu.make_async_copy(dq_in, dq, sem.at[0]),
        pltpu.make_async_copy(dkvr_in, dkvr, sem.at[1]),
        pltpu.make_async_copy(zr_in, zr, sem.at[2]),
    ]
    for cp in loads:
        cp.start()
    loads[0].wait()
    store = pltpu.make_async_copy(dq, dq_out, sem.at[3])
    store.start()
    loads[1].wait()
    loads[2].wait()
    t = lax.axis_index("tp")
    near = lax.rem(t, ZH)
    whole = jnp.where(jnp.logical_and(near == 1, lax.rem(t // ZH, 2) == 1), 0, 1)
    for h in range(8):
        over = jnp.where(whole == 1, dkvr[1 - near, h].astype(F32), 0.0)
        summed = dkvr[near, h].astype(F32) + over
        dk_out[:, h * HD : (h + 1) * HD] = summed[0].astype(BF16)
        dv_out[:, h * HD : (h + 1) * HD] = summed[1].astype(BF16)
    for w, ref in ((0, gpk_out), (1, gpv_out)):
        all_z = zr[w, 0].astype(F32)
        for i in range(1, 9):
            all_z = all_z + zr[w, i].astype(F32)
        ref[...] = all_z.astype(BF16)
    store.wait()


def body(queries, keys, values, out_grad, prefix_keys, prefix_values, lengths, prompt_of):
    dma = pltpu.SemaphoreType.DMA
    vm = lambda *shape: pltpu.VMEM(shape, BF16)
    out = lambda *shape: jax.ShapeDtypeStruct(shape, BF16)
    hbm = pl.BlockSpec(memory_space=pl.ANY)
    vmem = pl.BlockSpec(memory_space=pltpu.VMEM)
    wide = 2 * QW + 2 * HD
    dq, dkvr, zr = pl.pallas_call(
        kernel,
        out_shape=(out(TOK, 8 * REP * HD), out(2, 8, 2, TOK, HD), out(2, 9, 64, HD)),
        in_specs=[hbm] * 8,
        out_specs=(hbm,) * 3,
        scratch_shapes=[
            pltpu.SMEM((2,), jnp.int32),
            pltpu.SMEM((2,), jnp.int32),
            pltpu.VMEM((8, 128), jnp.int32),
            pltpu.VMEM((2, 8, 128), jnp.int32),
            pltpu.SMEM((2, 8, 128), jnp.int32),
            vm(TOK, 8 * QW),
            vm(TOK, 8 * QW),
            vm(TOK, 8 * HD),
            vm(TOK, 8 * HD),
            vm(8, TOK, wide),
            vm(2, 2, 4, TOK, HD),
            vm(8, TOK, wide),
            vm(2, 8, TOK, HD),
            vm(8, 4, 2, 64, HD),
            vm(8, 4, 2, 64, HD),
            vm(2, 4, 2, 4, 64, HD),
            vm(2, 8, 2, 4, 64, HD),
            vm(8, TOK, REP * HD),
            vm(2, 8, 2, TOK, HD),
            vm(2, 2, 2, 2, TOK, HD),
            vm(2, 4, 2, 64, HD),
            vm(2, 4, 2, 64, HD),
            vm(2, 4, 2, 64, HD),
            vm(2, 4, 2, 64, HD),
            vm(2, 4, 2, 64, HD),
            vm(2, 4, 2, 64, HD),
            vm(2, 8, 2, 64, HD),
            vm(2, 4, 2, 64, HD),
            vm(8, ROWS, HD),
            vm(8, ROWS, HD),
            vm(4, PLEN + RCAP, HD),
            vm(PLEN + RCAP, HD),
            pltpu.VMEM((2, PLEN + RCAP, ROWS), F32),
            pltpu.VMEM((2, PLEN + RCAP, ROWS), F32),
            pltpu.VMEM((8, PLEN + RCAP, ROWS), F32),
            vm(2, PLEN + RCAP, ROWS),
            vm(8, PLEN + RCAP, ROWS),
            dma((4,)),
            dma((4,)), dma((8,)), dma((8,)), dma((2, 2)), dma((2, 2)), dma((2, 8)), dma((2, 8)),
            pltpu.SemaphoreType.REGULAR((2,)), pltpu.SemaphoreType.REGULAR((2,)),
            dma((2, 5)), dma((2, 8, 2)),
            dma((2, 2, 3, 8)), dma((2, 8)), dma((2, 2, 8)), dma((2, 2, 8)), dma((2, 2, 8)), dma((2, 2, 8)),
            dma((8,)), dma((8,)), dma((8,)), dma((16,)), dma((2, 2, 2)), dma((2, 2, 2)), dma((2, 2, 4)), dma((2, 8)),
            dma((2, 4, 4)), dma((2, 4, 4)), dma((2, 2, 4)), dma((2, 2, 4)),
            dma((2, 2, 8)), dma((2, 9)), dma((2, 4)),
        ],
        compiler_params=pltpu.CompilerParams(
            collective_id=0, has_side_effects=True, vmem_limit_bytes=62 * 1024 * 1024
        ),
        cost_estimate=pl.CostEstimate(flops=2_000_000_000, bytes_accessed=4_000_000, transcendentals=1_400_000),
    )(queries, keys, values, out_grad, prefix_keys, prefix_values, lengths, prompt_of)
    return pl.pallas_call(
        finish,
        out_shape=(
            jax.ShapeDtypeStruct(queries.shape, BF16),
            jax.ShapeDtypeStruct(keys.shape, BF16),
            jax.ShapeDtypeStruct(values.shape, BF16),
            jax.ShapeDtypeStruct(prefix_keys.shape, BF16),
            jax.ShapeDtypeStruct(prefix_values.shape, BF16),
        ),
        in_specs=[hbm] * 3,
        out_specs=(hbm,) + (vmem,) * 4,
        scratch_shapes=[vm(TOK, 8 * REP * HD), vm(2, 8, 2, TOK, HD), vm(2, 9, 64, HD), dma((4,))],
        compiler_params=pltpu.CompilerParams(vmem_limit_bytes=62 * 1024 * 1024),
        name="finish",
    )(dq, dkvr, zr)


def solution(mesh):
    in_specs = (
        P(("resp", "tp"), None),
        P(("resp", "tp"), None),
        P(("resp", "tp"), None),
        P(("resp", "tp"), None),
        P("resp", "tp"),
        P("resp", "tp"),
        P("resp"),
        P("resp"),
    )
    out_specs = (
        P(("resp", "tp"), None),
        P(("resp", "tp"), None),
        P(("resp", "tp"), None),
        P("resp", "tp"),
        P("resp", "tp"),
    )
    return jax.shard_map(body, mesh=mesh, in_specs=in_specs, out_specs=out_specs, check_vma=False)
```

```python
import functools
import math

import jax
import jax.numpy as jnp
from jax import lax
from jax.experimental import pallas as pl
from jax.experimental.pallas import tpu as pltpu
from jax.sharding import PartitionSpec as P

HD = 128
RCAP = 128
PLEN = 512
PROMPTS = 8
X, Y, ZL, C, ZH = 4, 4, 8, 2, 2
Z = ZL * ZH
REP = 8
QW = REP * HD
LATE = 6
TOK = 32
MESH = pl.DeviceIdType.MESH
F32 = jnp.float32
BF16 = jnp.bfloat16
SCALE = 1.0 / math.sqrt(HD)
SCALE2 = SCALE * math.log2(math.e)


def where_is(x, y, z, c):
    return {"resp": x * (ZL * C) + lax.rem(z, ZL) * C + c, "tp": y * ZH + z // ZL}


def remote(src, dst, send, recv, device):
    return pltpu.make_async_remote_copy(
        src_ref=src, dst_ref=dst, send_sem=send, recv_sem=recv, device_id=device, device_id_type=MESH
    )


def dot_nt(a, b):
    return lax.dot_general(a, b, (((1,), (1,)), ((), ())), preferred_element_type=F32)


def dot_nn(a, b):
    return lax.dot_general(a, b, (((1,), (0,)), ((), ())), preferred_element_type=F32)


def dot_tn(a, b):
    return lax.dot_general(a, b, (((0,), (0,)), ((), ())), preferred_element_type=F32)


ROWS = REP * TOK
CHUNK = 128
CHUNKS = (PLEN + RCAP) // CHUNK


def kernel(
    q_in, k_in, v_in, g_in, pk_in, pv_in, len_in, prompt_in,
    dq_out, dkvr, zr,
    len_s, prompt_s, aux_l, aux_v, aux_s, qs, gs, ks, vs, side, kvrel, rows, kvx, pkb, pvb,
    term, dense, dqs, dkvs, dkrel,
    ra, rb, ra1, rb1, ra2, rb2, xsum, zrel, qh, gh, kk, vv, s_scr, dp_scr, p_scr, b_scr, ds_scr,
    aux_sem, in_sem, r_ss, r_rs, kr_ss, kr_rs, kx_ss, kx_rs,
    near_in, far_in, p_ss, p_rs, z_ss, z_rs, x_ss, x_rs, x2_ss, x2_rs,
    dq_ss, dq_rs, dkv_ss, dkv_rs, dr_ss, dr_rs, df_ss, df_rs,
    rx_ss, rx_rs, rx2_ss, rx2_rs, rz_ss, rz_rs, rl_rs,
):
    r = lax.axis_index("resp")
    t = lax.axis_index("tp")
    x, zl, c = r // (ZL * C), lax.rem(r // C, ZL), lax.rem(r, C)
    y, zh = t // ZH, lax.rem(t, ZH)
    z = zh * ZL + zl
    head = y * C + c
    xr, xl = lax.rem(x + 1, X), lax.rem(x + X - 1, X)
    xo = lax.rem(x + 2, X)
    zr_, zl_ = lax.rem(z + 1, Z), lax.rem(z + Z - 1, Z)
    here = where_is(x, y, z, c)

    z4 = (lax.rem(z + 4, Z), lax.rem(z + Z - 4, Z))
    y_odd = lax.rem(y, 2) == 1

    loads = [
        pltpu.make_async_copy(k_in, ks, in_sem.at[0]),
        pltpu.make_async_copy(v_in, vs, in_sem.at[1]),
        pltpu.make_async_copy(q_in, qs, in_sem.at[2]),
        pltpu.make_async_copy(g_in, gs, in_sem.at[3]),
    ]
    for cp in loads:
        cp.start()
    ints = [
        pltpu.make_async_copy(len_in, len_s, aux_sem.at[0]),
        pltpu.make_async_copy(prompt_in, prompt_s, aux_sem.at[3]),
    ]
    for cp in ints:
        cp.start()

    barrier = pltpu.get_barrier_semaphore()

    def greet(x_, y_, z_, c_):
        pl.semaphore_signal(barrier, inc=1, device_id=where_is(x_, y_, z_, c_), device_id_type=MESH)

    def greet_y(i, carry):
        y_ = lax.rem(y + i, Y)
        greet(x, y_, z, c)
        greet(x, y_, z, 1 - c)
        return carry

    lax.fori_loop(1, Y, greet_y, 0)
    greet(xr, y, z, c)
    greet(xl, y, z, c)
    greet(xo, y, z, c)
    greet(x, y, z, 1 - c)
    z2 = (lax.rem(z + 2, Z), lax.rem(z + Z - 2, Z))
    for z_ in (zr_, zl_) + z2:
        greet(x, y, z_, c)
        greet(x, y, z_, 1 - c)

    def tell(sem):
        for i in (0, 1):
            pl.semaphore_signal(sem.at[i], inc=1, device_id=where_is(x, y, z2[i], c), device_id_type=MESH)

    def told(sem):
        for i in (0, 1):
            pl.semaphore_wait(sem.at[i], 1)

    for cp in loads:
        cp.wait()
    for h in range(8):
        side[h, :, :QW] = qs[:, h * QW : (h + 1) * QW]
        side[h, :, QW : 2 * QW] = gs[:, h * QW : (h + 1) * QW]
        side[h, :, 2 * QW : 2 * QW + HD] = ks[:, h * HD : (h + 1) * HD]
        side[h, :, 2 * QW + HD :] = vs[:, h * HD : (h + 1) * HD]

    pl.semaphore_wait(barrier, 2 * (Y - 1) + 3 + 1 + 8)
    tell(near_in)

    def chunk(w, x_, zl_src):
        return prefix[w].at[x_ * 2 + zl_src // 4, lax.rem(zl_src, 4)]

    own_core = c == zh
    prefix_in = (pk_in, pv_in)
    prefix = (pkb, pvb)

    def mine_near(w):
        return pltpu.make_async_copy(prefix_in[w], chunk(w, x, zl).at[c], p_ss.at[w, 0])

    def mine_far(w, i):
        z_ = (z, zr_, z2[0], zl_, z2[1])[i]
        ref = chunk(w, x, zl).at[c]
        return remote(prefix_in[w], ref, p_ss.at[w, i], p_rs.at[w, zl, c], where_is(x, y, z_, zh))

    def mine_send(w):
        for i in (2, 4, 1, 3):
            mine_far(w, i).start()

        @pl.when(own_core)
        def _():
            mine_near(w).start()

        @pl.when(jnp.logical_not(own_core))
        def _():
            mine_far(w, 0).start()

    def halves_wait(w, s):
        for half in (0, 1):
            ref = chunk(w, x, s).at[half]
            remote(prefix_in[w], ref, p_ss.at[w, 0], p_rs.at[w, s, half], here).wait_recv()

    def mine_wait(w):
        @pl.when(own_core)
        def _():
            mine_near(w).wait()
            remote(prefix_in[w], chunk(w, x, zl).at[1 - c], p_ss.at[w, 0], p_rs.at[w, zl, 1 - c], here).wait_recv()

    mine_send(0)
    mine_send(1)

    def slot_of(y_, c_):
        return ((y_ // 2) * 2 + c_) * 2 + lax.rem(y_, 2)

    my_slot = slot_of(y, c)

    def row_copy(dy, dc):
        y_, c_ = lax.rem(y + dy, Y), lax.rem(c + dc, C)
        return remote(
            side.at[y_ * C + c_], rows.at[my_slot], r_ss.at[dy * 2 + dc], r_rs.at[my_slot], where_is(x, y_, z, c_)
        )

    def unseen(zh_src, odd):
        return jnp.logical_and(zh_src == 1, odd)

    def rel_copy(kv, way):
        src = side.at[pl.ds(4 * way, 4), :, pl.ds(2 * QW + kv * HD, HD)]
        return remote(src, kvrel.at[kv, way], kr_ss.at[kv, way], kr_rs.at[kv, way], where_is(x, y, z4[way], c))

    def rel_src(way):
        return z4[1 - way] // ZL

    def rel_on(kv, way):
        return [
            remote(
                kvrel.at[kv, way, i],
                kvx.at[kv, my_slot],
                kx_ss.at[kv, way * 4 + i],
                kx_rs.at[kv, my_slot],
                where_is(x, 2 * way + i // 2, z4[way], i % 2),
            )
            for i in range(4)
        ]

    def rel_start(kv):
        @pl.when(jnp.logical_not(unseen(zh, y_odd)))
        def _():
            for way in (0, 1):
                rel_copy(kv, way).start()

    def rel_pass(kv):
        for way in (0, 1):

            @pl.when(jnp.logical_not(unseen(rel_src(way), y_odd)))
            def _():
                rel_copy(kv, way).wait_recv()
                for cp in rel_on(kv, way):
                    cp.start()

    def kvx_wait(kv):
        for y_ in range(Y):
            for c_ in range(C):

                @pl.when(jnp.logical_not(unseen(1 - zh, y_ % 2 == 1)))
                def _():
                    ref = kvx.at[kv, slot_of(y_, c_)]
                    remote(ref, ref, kx_ss.at[kv, 0], kx_rs.at[kv, slot_of(y_, c_)], here).wait_recv()

    far = [(dy, dc) for dc in (0, 1) for dy in (1, 3, 2, 0) if (dy, dc) != (0, 0)]

    def y_start(*pairs):
        for dy, dc in pairs:
            row_copy(dy, dc).start()

    y_start((2, 0))
    own = pltpu.make_async_copy(side.at[head], rows.at[my_slot], r_ss.at[0])
    own.start()

    for cp in ints:
        cp.wait()
    lane = lax.broadcasted_iota(jnp.int32, (8, 128), 1)
    aux_l[...] = jnp.where(
        lane == 0,
        prompt_s[0],
        jnp.where(lane == 1, prompt_s[1], jnp.where(lane == 2, len_s[0], len_s[1])),
    )
    aux_own = pltpu.make_async_copy(aux_l, aux_v.at[c], aux_sem.at[0])
    aux_own.start()
    aux_far = remote(aux_l, aux_v.at[c], aux_sem.at[1], aux_sem.at[2], where_is(x, y, z, 1 - c))
    aux_far.start()

    def z_copy(w, way, far_, s):
        up_dev = where_is(x, y, lax.rem(z + 1 + far_, Z), c)
        down_dev = where_is(x, y, lax.rem(z + Z - 1 - far_, Z), c)
        ref = chunk(w, x, s)
        return remote(ref, ref, z_ss.at[w, way, far_, s], z_rs.at[w, s], up_dev if way == 0 else down_dev)

    def x_copy(w, way, s):
        ref, dev = chunk(w, x, s), where_is(xr if way == 0 else xl, y, z, c)
        return remote(ref, ref, x_ss.at[w, way, s], x_rs.at[w, way, s], dev)

    def x_arrived(w, way, s):
        ref = chunk(w, xl if way == 0 else xr, s)
        return remote(ref, ref, x_ss.at[w, way, s], x_rs.at[w, way, s], here)

    def x2_copy(w, way, s):
        ref, dev = chunk(w, xl if way == 0 else xr, s).at[way], where_is(xr if way == 0 else xl, y, z, c)
        return remote(ref, ref, x2_ss.at[w, way, s], x2_rs.at[w, way, s], dev)

    def x3_copy(w, s):
        ref = chunk(w, x, s)
        return remote(ref, ref, x2_ss.at[w, 0, s], x2_rs.at[w, 0, s], where_is(xo, y, z, c))

    def x3_arrived(w, s):
        ref = chunk(w, xo, s)
        return remote(ref, ref, x2_ss.at[w, 0, s], x2_rs.at[w, 0, s], here)

    def x2_arrived(w, way, s):
        ref = chunk(w, xo, s).at[way]
        return remote(ref, ref, x2_ss.at[w, way, s], x2_rs.at[w, way, s], here)

    def source(way, k):
        s = lax.rem(z + (Z - k if way == 0 else k), Z)
        return s // ZL == c, lax.rem(s, ZL)

    def x_start(w, s):
        x_copy(w, 0, s).start()
        x_copy(w, 1, s).start()

    def forwards(w, way, j, s):
        return [z_copy(w, way, i, s) for i in (2, 1, 0) if not (j == 2 and way == 1 and i == 2)]

    def stop(w, j):
        for way in (0, 1):
            live, s = source(way, 3 * j - 1 if j else 0)

            @pl.when(live)
            def _():
                if j == 1:
                    halves_wait(w, s)
                elif j == 2:
                    z_copy(w, way, 0, s).wait_recv()
                if j > 0:
                    for cp in forwards(w, way, j, s):
                        cp.start()

        for way in (0, 1):
            live, s = source(way, 3 * j - 1 if j else 0)

            @pl.when(live)
            def _():
                if j > 0 or way == 0:
                    x_start(w, s)

        for k in ((), (1,), (3, 4))[j]:
            for way in (0, 1):
                arrive(w, way, k)

    def arrive(w, way, k):
        live, s = source(way, k)

        @pl.when(live)
        def _():
            if k == 1:
                halves_wait(w, s)
            else:
                z_copy(w, way, 0, s).wait_recv()
            x_start(w, s)
            if k >= LATE:
                x3_copy(w, s).start()

    def stop_sent(w, j):
        for way in (0, 1):
            live, s = source(way, 3 * j - 1)

            @pl.when(live)
            def _():
                for cp in forwards(w, way, j, s):
                    cp.wait_send()

    def last_arrivals(w):
        for way, k in ((0, 6), (1, 6), (0, 7), (1, 7), (0, 8)):
            arrive(w, way, k)

    def pass_on(w, way, k):
        live, s = source(way, k)

        @pl.when(live)
        def _():
            for x_way in (0, 1):
                x_arrived(w, x_way, s).wait_recv()
                x2_copy(w, x_way, s).start()

    def all_on(w, low, high):
        for k in range(low, high):
            pass_on(w, 0, k)
            if 0 < k < 8:
                pass_on(w, 1, k)

    all_sources = [(way, k) for k in range(9) for way in (0, 1) if way == 0 or 0 < k < 8]

    def x2_wait(w):
        for way, k in all_sources:
            live, s = source(way, k)

            @pl.when(live)
            def _():
                if k >= LATE:
                    x_arrived(w, 0, s).wait_recv()
                    x_arrived(w, 1, s).wait_recv()
                    x3_arrived(w, s).wait_recv()
                else:
                    x2_arrived(w, 0, s).wait_recv()
                    x2_arrived(w, 1, s).wait_recv()

    mine_wait(0)
    stop(0, 0)
    y_start((1, 0))
    mine_wait(1)
    told(near_in)
    tell(far_in)
    stop(0, 1)
    stop(1, 0)
    told(far_in)
    rel_start(0)
    y_start((2, 1), (3, 0))
    stop(0, 2)
    stop(1, 1)
    rel_pass(0)
    rel_start(1)
    y_start((1, 1), (3, 1))
    all_on(0, 0, 3)
    last_arrivals(0)
    stop(1, 2)
    all_on(0, 3, LATE)
    y_start((0, 1))
    rel_pass(1)
    last_arrivals(1)
    all_on(1, 0, 3)

    for dy, dc in far:
        ref = rows.at[slot_of(lax.rem(y + dy, Y), lax.rem(c + dc, C))]
        remote(ref, ref, r_ss.at[0], r_rs.at[slot_of(lax.rem(y + dy, Y), lax.rem(c + dc, C))], here).wait_recv()
    kvx_wait(0)
    own.wait()
    aux_own.wait()
    remote(aux_l, aux_v.at[1 - c], aux_sem.at[1], aux_sem.at[2], here).wait_recv()

    to_smem = pltpu.make_async_copy(aux_v, aux_s, aux_sem.at[3])
    to_smem.start()
    to_smem.wait()

    x2_wait(0)

    def q_cols(ref, h):
        return ref.at[:, pl.ds(pl.multiple_of(h * QW, QW), QW)]

    def dq_copy(sl):
        rho = sl // 2
        y_, c_ = (rho // 2) * 2 + lax.rem(sl, 2), lax.rem(rho, 2)
        dst = q_cols(dq_out, head)
        return (
            sl == my_slot,
            remote(dqs.at[sl], dst, dq_ss.at[sl], dq_rs.at[head], where_is(x, y_, z, c_)),
            pltpu.make_async_copy(dqs.at[sl], dst, dq_ss.at[sl]),
        )

    def dkv_copy(rho, yb):
        y_, c_ = (rho // 2) * 2 + yb, lax.rem(rho, 2)
        i = dk_slot(rho, yb)
        src, dst = dkvs.at[zh, i], dkvr.at[zh, head]
        return (
            jnp.logical_and(y_ == y, c_ == c),
            remote(src, dst, dkv_ss.at[i], dkv_rs.at[zh * 8 + head], where_is(x, y_, z, c_)),
            pltpu.make_async_copy(src, dst, dkv_ss.at[i]),
        )

    def dk_slot(rho, yb):
        return (rho // 2) * 4 + yb * 2 + lax.rem(rho, 2)

    def drel_copy(kv, way, yb):
        dev = where_is(x, y, jnp.where(way == 0, z4[0], z4[1]), c)
        src = dkvs.at[1 - zh, pl.ds(way * 4 + yb * 2, 2), kv]
        return remote(src, dkrel.at[kv, way, yb], dr_ss.at[kv, way, yb], dr_rs.at[kv, way, yb], dev)

    def drel_start(kv, way):
        drel_copy(kv, way, 0).start()

        @pl.when(zh == 1)
        def _():
            drel_copy(kv, way, 1).start()

    def drel_on(kv, way, yb):
        zs = rel_src(way)
        return [
            remote(
                dkrel.at[kv, way, yb, i],
                dkvr.at[zs, head, kv],
                df_ss.at[kv, way, yb * 2 + i],
                df_rs.at[kv, head],
                where_is(x, 2 * way + yb, z4[way], i),
            )
            for i in (0, 1)
        ]

    def drel_pass(kv, way):
        drel_copy(kv, way, 0).wait_recv()
        for cp in drel_on(kv, way, 0):
            cp.start()

        @pl.when(rel_src(way) == 1)
        def _():
            drel_copy(kv, way, 1).wait_recv()
            for cp in drel_on(kv, way, 1):
                cp.start()

    def send(copies):
        local, far_cp, near_cp = copies

        @pl.when(local)
        def _():
            near_cp.start()

        @pl.when(jnp.logical_not(local))
        def _():
            far_cp.start()

    def sent(copies):
        local, far_cp, near_cp = copies

        @pl.when(local)
        def _():
            near_cp.wait()

        @pl.when(jnp.logical_not(local))
        def _():
            far_cp.wait_send()

    def fold(a, op):
        return op(a.reshape(CHUNK // 8, 8, ROWS), 0)

    def keys_of(kv, prompt, rho, to):
        to[:PLEN] = prefix[kv][prompt].reshape(PLEN, HD)
        for b in (0, 1):
            i = rho * 2 + b
            near = pl.ds(pl.multiple_of(PLEN + (2 * b + zh) * TOK, TOK), TOK)
            over = pl.ds(pl.multiple_of(PLEN + (2 * b + 1 - zh) * TOK, TOK), TOK)
            low = 2 * QW + kv * HD
            to[near] = rows[i, :, low : low + HD]
            crossed = kvx[kv, i].astype(F32)
            if b == 1:
                crossed = jnp.where(zh == 1, crossed, 0.0)
            to[over] = crossed.astype(BF16)

    def leave(kv, rho, grad):
        for i in range(4):
            for ct in (0, 1):
                low = (i * 2 + ct) * 64
                term[kv, rho, ct, i] = grad[low : low + 64].astype(BF16)
        for tb in range(4):
            low = PLEN + tb * TOK
            dkvs[tb % 2, dk_slot(rho, tb // 2), kv] = grad[low : low + TOK].astype(BF16)

    def weigh(rho, carry):
        prompt = aux_s[lax.rem(rho, 2), 0, rho // 2]
        length = aux_s[lax.rem(rho, 2), 0, 2 + rho // 2]
        k_rho = kk.at[rho]
        keys_of(0, prompt, rho, k_rho)
        acc = []
        for b in (0, 1):
            i = rho * 2 + b
            qa, ga = rows[i, :, :QW], rows[i, :, QW : 2 * QW]
            tok = lax.broadcasted_iota(jnp.int32, (TOK, HD), 0) + (64 * b + TOK * zh)
            keep = jnp.where(tok < length, 1.0, 0.0)
            q = jnp.concatenate([qa[:, h * HD : (h + 1) * HD] for h in range(REP)], axis=0)
            g = jnp.concatenate(
                [(ga[:, h * HD : (h + 1) * HD].astype(F32) * keep).astype(BF16) for h in range(REP)], axis=0
            )
            qh[i] = q
            gh[i] = g
            top = jnp.full((8, ROWS), -jnp.inf, F32)
            for n in range(CHUNKS):
                at = slice(n * CHUNK, (n + 1) * CHUNK)
                s = dot_nt(k_rho[at], q)
                if n == CHUNKS - 1:
                    col = lax.broadcasted_iota(jnp.int32, (CHUNK, ROWS), 1)
                    key = lax.broadcasted_iota(jnp.int32, (CHUNK, ROWS), 0)
                    s = jnp.where(key <= lax.rem(col, TOK) + (64 * b + TOK * zh), s, -jnp.inf)
                s_scr[b, at] = s
                top = jnp.maximum(top, fold(s, jnp.max))
            top = jnp.max(top, 0, keepdims=True)
            total = jnp.zeros((8, ROWS), F32)
            for n in range(CHUNKS):
                at = slice(n * CHUNK, (n + 1) * CHUNK)
                e = jnp.exp2((s_scr[b, at] - top) * SCALE2)
                s_scr[b, at] = e
                total = total + fold(e, jnp.sum)
            inv = 1.0 / jnp.sum(total, 0, keepdims=True)
            for n in range(CHUNKS):
                at = slice(n * CHUNK, (n + 1) * CHUNK)
                p = s_scr[b, at] * inv
                p_scr[i, at] = p
                b_scr[b, at] = p.astype(BF16)
            acc.append(dot_nn(b_scr[b], g))
        leave(1, rho, acc[0] + acc[1])

        @pl.when(lax.rem(rho, 2) == 1)
        def _():
            drel_start(1, rho // 2)

        @pl.when(rho == 0)
        def _():
            all_on(1, 3, LATE)

        return carry

    def differentiate(rho, carry):
        prompt = aux_s[lax.rem(rho, 2), 0, rho // 2]
        keys_of(1, prompt, rho, vv)
        acc = []
        for b in (0, 1):
            i = rho * 2 + b
            mixed = jnp.zeros((8, ROWS), F32)
            for n in range(CHUNKS):
                at = slice(n * CHUNK, (n + 1) * CHUNK)
                dp = dot_nt(vv[at], gh[i])
                dp_scr[b, at] = dp
                mixed = mixed + fold(p_scr[i, at] * dp, jnp.sum)
            delta = jnp.sum(mixed, 0, keepdims=True)
            for n in range(CHUNKS):
                at = slice(n * CHUNK, (n + 1) * CHUNK)
                ds_scr[i, at] = (p_scr[i, at] * (dp_scr[b, at] - delta)).astype(BF16)
            acc.append(dot_nn(ds_scr[i], qh[i]))
        leave(0, rho, (acc[0] + acc[1]) * SCALE)

        @pl.when(lax.rem(rho, 2) == 1)
        def _():
            drel_start(0, rho // 2)

        for b in (0, 1):
            send(dkv_copy(rho, b))

        @pl.when(rho == 2)
        def _():
            for way in (0, 1):
                drel_pass(1, way)

        first(1, order(rho))

        @pl.when(rho >= 2)
        def _():
            second(1, order(rho - 2))

        return carry

    def query_grads(rho, carry):
        for b in (0, 1):
            i = rho * 2 + b
            dq = (dot_tn(kk[rho], ds_scr[i]) * SCALE).T.astype(BF16)
            for h in range(REP):
                dqs[i, :, h * HD : (h + 1) * HD] = dq[h * TOK : (h + 1) * TOK]
        return carry

    def part(w, x_, n, half):
        return dense.at[w, x_ * 2 + n // 2, half, pl.ds(lax.rem(n, 2) * 2, 2)]

    def own_part(w, x_, n, half):
        return dense[w, x_ * 2 + n // 2, half, pl.ds(lax.rem(n, 2) * 2, 2)].astype(F32)

    def rx_copy(w, way, n):
        if way == 0:
            src, dst, dev = part(w, xo, n, 0), ra.at[w, n], where_is(xr, y, z, c)
        elif way == 1:
            src, dst, dev = part(w, xo, n, 1), rb.at[w, n], where_is(xl, y, z, c)
        elif way == 2:
            src, dst, dev = part(w, xr, n, 1), rb1.at[w, n], where_is(xr, y, z, c)
        else:
            src, dst, dev = part(w, xl, n, 0), ra1.at[w, n], where_is(xl, y, z, c)
        return remote(src, dst, rx_ss.at[w, way, n], rx_rs.at[w, way, n], dev)

    def rx2_copy(w, way, n):
        if way == 0:
            src, dst, dev = ra.at[w, n], ra2.at[w, n], where_is(xr, y, z, c)
        else:
            src, dst, dev = rb.at[w, n], rb2.at[w, n], where_is(xl, y, z, c)
        return remote(src, dst, rx2_ss.at[w, way, n], rx2_rs.at[w, way, n], dev)

    rising = (zh != c) == (zl < 4)

    def order(i):
        n = lax.rem(i, 2) * 2 + i // 2
        return jnp.where(rising, n, 3 - n)

    def spread_all(w):
        def spread_half(i, carry):
            ip = jnp.where(rising, i, 1 - i)
            two = pl.ds(ip * 2, 2)

            def spread(p, carry):
                acc = jnp.zeros((2, 2, 64, HD), F32)
                for rho in range(4):
                    hit = aux_s[rho % 2, 0, rho // 2] == p
                    acc = acc + jnp.where(hit, term[w, rho, :, two].astype(F32), 0.0)
                dense[w, p, :, two] = acc.astype(BF16)
                return carry

            lax.fori_loop(0, PROMPTS, spread, 0)
            for j in (0, 1):
                for way in (0, 1):
                    rx_copy(w, way, order(2 * i + j)).start()
            return carry

        lax.fori_loop(0, 2, spread_half, 0)

    def z_dist(zt):
        return lax.rem(c * ZL + zt - z + 23, Z) - 7

    def z_direct(w, zt, ct, d):
        src, dst, zd = xsum.at[w, zt, ct], zr.at[w, d + 4], c * ZL + zt
        return (
            jnp.logical_and(d == 0, ct == c),
            remote(src, dst, rz_ss.at[w, ct, zt], rz_rs.at[w, d + 4], where_is(x, y, zd, ct)),
            pltpu.make_async_copy(src, dst, rz_ss.at[w, ct, zt]),
        )

    def z_stop(w, zt, d):
        up_ = d > 0
        zd = lax.rem(z + Z + jnp.where(up_, d - 4, d + 4), Z)
        i = jnp.where(up_, d, -d) - 5
        return remote(xsum.at[w, zt], zrel.at[w, i], rz_ss.at[w, 0, zt], rl_rs.at[w, i], where_is(x, y, zd, c))

    def is_far(d):
        return jnp.logical_or(d > 4, d < -4)

    def is_near(d):
        return jnp.logical_and(d < 4, d > -4)

    def first(w, n):
        rx_copy(w, 0, n).wait_recv()
        ra[w, n] = (ra[w, n].astype(F32) + own_part(w, xr, n, 0)).astype(BF16)
        rx2_copy(w, 0, n).start()
        rx_copy(w, 1, n).wait_recv()
        rb[w, n] = (rb[w, n].astype(F32) + own_part(w, xl, n, 1)).astype(BF16)
        rx2_copy(w, 1, n).start()
        rx_copy(w, 2, n).start()
        rx_copy(w, 3, n).start()

    def second(w, n):
        rx_copy(w, 3, n).wait_recv()
        rx2_copy(w, 0, n).wait_recv()
        one = own_part(w, x, n, 0) + ra1[w, n].astype(F32) + ra2[w, n].astype(F32)
        rx_copy(w, 2, n).wait_recv()
        rx2_copy(w, 1, n).wait_recv()
        two = own_part(w, x, n, 1) + rb1[w, n].astype(F32) + rb2[w, n].astype(F32)
        for i in (0, 1):
            zt = 2 * n + i
            xsum[w, zt, 0] = one[i].astype(BF16)
            xsum[w, zt, 1] = two[i].astype(BF16)
            d = z_dist(zt)

            @pl.when(is_near(d))
            def _():
                for ct in (0, 1):
                    send(z_direct(w, zt, ct, d))

            @pl.when(is_far(d))
            def _():
                z_stop(w, zt, d).start()

    zt_stop = lax.rem(zl + 4, ZL)
    d_stop = z_dist(zt_stop)

    def stop_sum(w):
        def stop_wait(i, carry):
            @pl.when(jnp.logical_or(i < 3, d_stop > 0))
            def _():
                remote(zrel.at[w, i], zrel.at[w, i], rz_ss.at[w, 0, 0], rl_rs.at[w, i], here).wait_recv()

            return carry

        lax.fori_loop(0, 4, stop_wait, 0)
        for ct in (0, 1):
            three = xsum[w, zt_stop, ct].astype(F32)
            for i in range(3):
                three = three + zrel[w, i, ct].astype(F32)

            @pl.when(d_stop > 0)
            def _():
                xsum[w, zt_stop, ct] = (three + zrel[w, 3, ct].astype(F32)).astype(BF16)

            @pl.when(d_stop < 0)
            def _():
                xsum[w, zt_stop, ct] = three.astype(BF16)

            z_direct(w, zt_stop, ct, d_stop)[1].start()

    lax.fori_loop(0, 4, weigh, 0)
    spread_all(1)
    x2_wait(1)
    kvx_wait(1)
    lax.fori_loop(0, 4, differentiate, 0)
    spread_all(0)
    drel_pass(0, 0)
    lax.fori_loop(0, 4, query_grads, 0)
    second(1, order(2))
    second(1, order(3))

    def last(i, carry):
        @pl.when(i < 4)
        def _():
            first(0, order(i))
            send(dq_copy(2 * i))
            send(dq_copy(2 * i + 1))

        @pl.when(i == 1)
        def _():
            drel_pass(0, 1)

        @pl.when(i == 2)
        def _():
            stop_sum(1)

        @pl.when(i >= 1)
        def _():
            second(0, order(i - 1))

        return carry

    lax.fori_loop(0, 5, last, 0)
    stop_sum(0)

    def dkv_wait(h, carry):
        near = dkvr.at[zh, h]

        @pl.when(h != head)
        def _():
            remote(near, near, dkv_ss.at[0], dkv_rs.at[zh * 8 + h], here).wait_recv()

        @pl.when(jnp.logical_not(unseen(zh, y_odd)))
        def _():
            for kv in (0, 1):
                over = dkvr.at[1 - zh, h, kv]
                remote(over, over, dkv_ss.at[0], df_rs.at[kv, h], here).wait_recv()

        return carry

    def dkv_sent(i, carry):
        for yb in (0, 1):
            sent(dkv_copy(i, yb))
        return carry

    lax.fori_loop(0, 4, dkv_sent, 0)
    lax.fori_loop(0, 8, dkv_wait, 0)
    def z_sent(i, carry):
        w, n = i // ZL, lax.rem(i, ZL)
        d = z_dist(n)

        @pl.when(is_far(d))
        def _():
            z_stop(w, n, d).wait_send()

        @pl.when(jnp.logical_not(is_far(d)))
        def _():
            for ct in (0, 1):
                sent(z_direct(w, n, ct, d))

        return carry

    def z_wait(i, carry):
        for w in (0, 1):

            @pl.when(jnp.logical_not(jnp.logical_and(own_core, i == 4)))
            def _():
                remote(zr.at[w, i], zr.at[w, i], rz_ss.at[w, 0, 0], rz_rs.at[w, i], here).wait_recv()

        return carry

    lax.fori_loop(0, 2 * ZL, z_sent, 0)
    lax.fori_loop(0, 9, z_wait, 0)

    def dq_wait(h, carry):
        @pl.when(h != head)
        def _():
            ref = q_cols(dq_out, h)
            remote(ref, ref, dq_ss.at[0], dq_rs.at[h], here).wait_recv()

        return carry

    def dq_sent(i, carry):
        sent(dq_copy(i))
        return carry

    lax.fori_loop(0, 8, dq_sent, 0)
    lax.fori_loop(0, 8, dq_wait, 0)
    aux_far.wait_send()
    for dy, dc in far:
        row_copy(dy, dc).wait_send()

    @pl.when(jnp.logical_not(unseen(zh, y_odd)))
    def _():
        for kv in (0, 1):
            for way in (0, 1):
                rel_copy(kv, way).wait_send()

    for way in (0, 1):

        @pl.when(jnp.logical_not(unseen(rel_src(way), y_odd)))
        def _():
            for cp in rel_on(0, way) + rel_on(1, way):
                cp.wait_send()

        for kv in (0, 1):
            drel_copy(kv, way, 0).wait_send()
            for cp in drel_on(kv, way, 0):
                cp.wait_send()

        @pl.when(zh == 1)
        def _():
            for kv in (0, 1):
                drel_copy(kv, way, 1).wait_send()

        @pl.when(rel_src(way) == 1)
        def _():
            for kv in (0, 1):
                for cp in drel_on(kv, way, 1):
                    cp.wait_send()

    for w in (0, 1):
        for i in (1, 2, 3, 4):
            mine_far(w, i).wait_send()

        @pl.when(jnp.logical_not(own_core))
        def _():
            mine_far(w, 0).wait_send()

    for w in (0, 1):
        for j in (1, 2):
            stop_sent(w, j)

    def x_sent(s, carry):
        for w in (0, 1):
            for way in (0, 1):
                x_copy(w, way, s).wait_send()
        return carry

    lax.fori_loop(0, ZL, x_sent, 0)
    for w in (0, 1):
        for way, k in all_sources:
            live, s = source(way, k)

            @pl.when(live)
            def _():
                if k >= LATE:
                    x3_copy(w, s).wait_send()
                else:
                    x2_copy(w, 0, s).wait_send()
                    x2_copy(w, 1, s).wait_send()

    def rx_sent(n, carry):
        for w in (0, 1):
            for way in range(4):
                rx_copy(w, way, n).wait_send()
            for way in (0, 1):
                rx2_copy(w, way, n).wait_send()
        return carry

    lax.fori_loop(0, 4, rx_sent, 0)


def finish(dq_in, dkvr_in, zr_in, dq_out, dk_out, dv_out, gpk_out, gpv_out, dq, dkvr, zr, sem):
    loads = [
        pltpu.make_async_copy(dq_in, dq, sem.at[0]),
        pltpu.make_async_copy(dkvr_in, dkvr, sem.at[1]),
        pltpu.make_async_copy(zr_in, zr, sem.at[2]),
    ]
    for cp in loads:
        cp.start()
    loads[0].wait()
    store = pltpu.make_async_copy(dq, dq_out, sem.at[3])
    store.start()
    loads[1].wait()
    loads[2].wait()
    t = lax.axis_index("tp")
    near = lax.rem(t, ZH)
    whole = jnp.where(jnp.logical_and(near == 1, lax.rem(t // ZH, 2) == 1), 0, 1)
    for h in range(8):
        over = jnp.where(whole == 1, dkvr[1 - near, h].astype(F32), 0.0)
        summed = dkvr[near, h].astype(F32) + over
        dk_out[:, h * HD : (h + 1) * HD] = summed[0].astype(BF16)
        dv_out[:, h * HD : (h + 1) * HD] = summed[1].astype(BF16)
    for w, ref in ((0, gpk_out), (1, gpv_out)):
        all_z = zr[w, 0].astype(F32)
        for i in range(1, 9):
            all_z = all_z + zr[w, i].astype(F32)
        ref[...] = all_z.astype(BF16)
    store.wait()


def body(queries, keys, values, out_grad, prefix_keys, prefix_values, lengths, prompt_of):
    dma = pltpu.SemaphoreType.DMA
    vm = lambda *shape: pltpu.VMEM(shape, BF16)
    out = lambda *shape: jax.ShapeDtypeStruct(shape, BF16)
    hbm = pl.BlockSpec(memory_space=pl.ANY)
    vmem = pl.BlockSpec(memory_space=pltpu.VMEM)
    wide = 2 * QW + 2 * HD
    dq, dkvr, zr = pl.pallas_call(
        kernel,
        out_shape=(out(TOK, 8 * REP * HD), out(2, 8, 2, TOK, HD), out(2, 9, 64, HD)),
        in_specs=[hbm] * 8,
        out_specs=(hbm,) * 3,
        scratch_shapes=[
            pltpu.SMEM((2,), jnp.int32),
            pltpu.SMEM((2,), jnp.int32),
            pltpu.VMEM((8, 128), jnp.int32),
            pltpu.VMEM((2, 8, 128), jnp.int32),
            pltpu.SMEM((2, 8, 128), jnp.int32),
            vm(TOK, 8 * QW),
            vm(TOK, 8 * QW),
            vm(TOK, 8 * HD),
            vm(TOK, 8 * HD),
            vm(8, TOK, wide),
            vm(2, 2, 4, TOK, HD),
            vm(8, TOK, wide),
            vm(2, 8, TOK, HD),
            vm(8, 4, 2, 64, HD),
            vm(8, 4, 2, 64, HD),
            vm(2, 4, 2, 4, 64, HD),
            vm(2, 8, 2, 4, 64, HD),
            vm(8, TOK, REP * HD),
            vm(2, 8, 2, TOK, HD),
            vm(2, 2, 2, 2, TOK, HD),
            vm(2, 4, 2, 64, HD),
            vm(2, 4, 2, 64, HD),
            vm(2, 4, 2, 64, HD),
            vm(2, 4, 2, 64, HD),
            vm(2, 4, 2, 64, HD),
            vm(2, 4, 2, 64, HD),
            vm(2, 8, 2, 64, HD),
            vm(2, 4, 2, 64, HD),
            vm(8, ROWS, HD),
            vm(8, ROWS, HD),
            vm(4, PLEN + RCAP, HD),
            vm(PLEN + RCAP, HD),
            pltpu.VMEM((2, PLEN + RCAP, ROWS), F32),
            pltpu.VMEM((2, PLEN + RCAP, ROWS), F32),
            pltpu.VMEM((8, PLEN + RCAP, ROWS), F32),
            vm(2, PLEN + RCAP, ROWS),
            vm(8, PLEN + RCAP, ROWS),
            dma((4,)),
            dma((4,)), dma((8,)), dma((8,)), dma((2, 2)), dma((2, 2)), dma((2, 8)), dma((2, 8)),
            pltpu.SemaphoreType.REGULAR((2,)), pltpu.SemaphoreType.REGULAR((2,)),
            dma((2, 5)), dma((2, 8, 2)),
            dma((2, 2, 3, 8)), dma((2, 8)), dma((2, 2, 8)), dma((2, 2, 8)), dma((2, 2, 8)), dma((2, 2, 8)),
            dma((8,)), dma((8,)), dma((8,)), dma((16,)), dma((2, 2, 2)), dma((2, 2, 2)), dma((2, 2, 4)), dma((2, 8)),
            dma((2, 4, 4)), dma((2, 4, 4)), dma((2, 2, 4)), dma((2, 2, 4)),
            dma((2, 2, 8)), dma((2, 9)), dma((2, 4)),
        ],
        compiler_params=pltpu.CompilerParams(
            collective_id=0, has_side_effects=True, vmem_limit_bytes=62 * 1024 * 1024
        ),
        cost_estimate=pl.CostEstimate(flops=2_000_000_000, bytes_accessed=4_000_000, transcendentals=1_400_000),
    )(queries, keys, values, out_grad, prefix_keys, prefix_values, lengths, prompt_of)
    return pl.pallas_call(
        finish,
        out_shape=(
            jax.ShapeDtypeStruct(queries.shape, BF16),
            jax.ShapeDtypeStruct(keys.shape, BF16),
            jax.ShapeDtypeStruct(values.shape, BF16),
            jax.ShapeDtypeStruct(prefix_keys.shape, BF16),
            jax.ShapeDtypeStruct(prefix_values.shape, BF16),
        ),
        in_specs=[hbm] * 3,
        out_specs=(hbm,) + (vmem,) * 4,
        scratch_shapes=[vm(TOK, 8 * REP * HD), vm(2, 8, 2, TOK, HD), vm(2, 9, 64, HD), dma((4,))],
        compiler_params=pltpu.CompilerParams(vmem_limit_bytes=62 * 1024 * 1024),
        name="finish",
    )(dq, dkvr, zr)


def solution(mesh):
    in_specs = (
        P(("resp", "tp"), None),
        P(("resp", "tp"), None),
        P(("resp", "tp"), None),
        P(("resp", "tp"), None),
        P("resp", "tp"),
        P("resp", "tp"),
        P("resp"),
        P("resp"),
    )
    out_specs = (
        P(("resp", "tp"), None),
        P(("resp", "tp"), None),
        P(("resp", "tp"), None),
        P("resp", "tp"),
        P("resp", "tp"),
    )
    return jax.shard_map(body, mesh=mesh, in_specs=in_specs, out_specs=out_specs, check_vma=False)
```

```python
import functools
import math

import jax
import jax.numpy as jnp
from jax import lax
from jax.experimental import pallas as pl
from jax.experimental.pallas import tpu as pltpu
from jax.sharding import PartitionSpec as P

HD = 128
RCAP = 128
PLEN = 512
PROMPTS = 8
X, Y, ZL, C, ZH = 4, 4, 8, 2, 2
Z = ZL * ZH
REP = 8
QW = REP * HD
LATE = 6
TOK = 32
MESH = pl.DeviceIdType.MESH
F32 = jnp.float32
BF16 = jnp.bfloat16
SCALE = 1.0 / math.sqrt(HD)
SCALE2 = SCALE * math.log2(math.e)


def where_is(x, y, z, c):
    return {"resp": x * (ZL * C) + lax.rem(z, ZL) * C + c, "tp": y * ZH + z // ZL}


def remote(src, dst, send, recv, device):
    return pltpu.make_async_remote_copy(
        src_ref=src, dst_ref=dst, send_sem=send, recv_sem=recv, device_id=device, device_id_type=MESH
    )


def dot_nt(a, b):
    return lax.dot_general(a, b, (((1,), (1,)), ((), ())), preferred_element_type=F32)


def dot_nn(a, b):
    return lax.dot_general(a, b, (((1,), (0,)), ((), ())), preferred_element_type=F32)


def dot_tn(a, b):
    return lax.dot_general(a, b, (((0,), (0,)), ((), ())), preferred_element_type=F32)


ROWS = REP * TOK
CHUNK = 128
CHUNKS = (PLEN + RCAP) // CHUNK


def kernel(
    q_in, k_in, v_in, g_in, pk_in, pv_in, len_in, prompt_in,
    dq_out, dkvr, zr,
    len_s, prompt_s, aux_l, aux_v, aux_s, qs, gs, ks, vs, side, kvrel, rows, kvx, pkb, pvb,
    term, dense, dqs, dkvs, dkrel,
    ra, rb, ra1, rb1, ra2, rb2, xsum, zrel, qh, gh, kk, vv, s_scr, dp_scr, p_scr, b_scr, ds_scr,
    aux_sem, in_sem, r_ss, r_rs, kr_ss, kr_rs, kx_ss, kx_rs,
    near_in, far_in, p_ss, p_rs, z_ss, z_rs, x_ss, x_rs, x2_ss, x2_rs,
    dq_ss, dq_rs, dkv_ss, dkv_rs, dr_ss, dr_rs, df_ss, df_rs,
    rx_ss, rx_rs, rx2_ss, rx2_rs, rz_ss, rz_rs, rl_rs,
):
    r = lax.axis_index("resp")
    t = lax.axis_index("tp")
    x, zl, c = r // (ZL * C), lax.rem(r // C, ZL), lax.rem(r, C)
    y, zh = t // ZH, lax.rem(t, ZH)
    z = zh * ZL + zl
    head = y * C + c
    xr, xl = lax.rem(x + 1, X), lax.rem(x + X - 1, X)
    xo = lax.rem(x + 2, X)
    zr_, zl_ = lax.rem(z + 1, Z), lax.rem(z + Z - 1, Z)
    here = where_is(x, y, z, c)

    z4 = (lax.rem(z + 4, Z), lax.rem(z + Z - 4, Z))
    y_odd = lax.rem(y, 2) == 1

    loads = [
        pltpu.make_async_copy(k_in, ks, in_sem.at[0]),
        pltpu.make_async_copy(v_in, vs, in_sem.at[1]),
        pltpu.make_async_copy(q_in, qs, in_sem.at[2]),
        pltpu.make_async_copy(g_in, gs, in_sem.at[3]),
    ]
    for cp in loads:
        cp.start()
    ints = [
        pltpu.make_async_copy(len_in, len_s, aux_sem.at[0]),
        pltpu.make_async_copy(prompt_in, prompt_s, aux_sem.at[3]),
    ]
    for cp in ints:
        cp.start()

    barrier = pltpu.get_barrier_semaphore()

    def greet(x_, y_, z_, c_):
        pl.semaphore_signal(barrier, inc=1, device_id=where_is(x_, y_, z_, c_), device_id_type=MESH)

    def greet_y(i, carry):
        y_ = lax.rem(y + i, Y)
        greet(x, y_, z, c)
        greet(x, y_, z, 1 - c)
        return carry

    lax.fori_loop(1, Y, greet_y, 0)
    greet(xr, y, z, c)
    greet(xl, y, z, c)
    greet(xo, y, z, c)
    greet(x, y, z, 1 - c)
    z2 = (lax.rem(z + 2, Z), lax.rem(z + Z - 2, Z))
    for z_ in (zr_, zl_) + z2:
        greet(x, y, z_, c)
        greet(x, y, z_, 1 - c)

    def tell(sem):
        for i in (0, 1):
            pl.semaphore_signal(sem.at[i], inc=1, device_id=where_is(x, y, z2[i], c), device_id_type=MESH)

    def told(sem):
        for i in (0, 1):
            pl.semaphore_wait(sem.at[i], 1)

    for cp in loads:
        cp.wait()
    for h in range(8):
        side[h, :, :QW] = qs[:, h * QW : (h + 1) * QW]
        side[h, :, QW : 2 * QW] = gs[:, h * QW : (h + 1) * QW]
        side[h, :, 2 * QW : 2 * QW + HD] = ks[:, h * HD : (h + 1) * HD]
        side[h, :, 2 * QW + HD :] = vs[:, h * HD : (h + 1) * HD]

    pl.semaphore_wait(barrier, 2 * (Y - 1) + 3 + 1 + 8)
    tell(near_in)

    def chunk(w, x_, zl_src):
        return prefix[w].at[x_ * 2 + zl_src // 4, lax.rem(zl_src, 4)]

    own_core = c == zh
    prefix_in = (pk_in, pv_in)
    prefix = (pkb, pvb)

    def mine_near(w):
        return pltpu.make_async_copy(prefix_in[w], chunk(w, x, zl).at[c], p_ss.at[w, 0])

    def mine_far(w, i):
        z_ = (z, zr_, z2[0], zl_, z2[1])[i]
        ref = chunk(w, x, zl).at[c]
        return remote(prefix_in[w], ref, p_ss.at[w, i], p_rs.at[w, zl, c], where_is(x, y, z_, zh))

    def mine_send(w):
        for i in (2, 4, 1, 3):
            mine_far(w, i).start()

        @pl.when(own_core)
        def _():
            mine_near(w).start()

        @pl.when(jnp.logical_not(own_core))
        def _():
            mine_far(w, 0).start()

    def halves_wait(w, s):
        for half in (0, 1):
            ref = chunk(w, x, s).at[half]
            remote(prefix_in[w], ref, p_ss.at[w, 0], p_rs.at[w, s, half], here).wait_recv()

    def mine_wait(w):
        @pl.when(own_core)
        def _():
            mine_near(w).wait()
            remote(prefix_in[w], chunk(w, x, zl).at[1 - c], p_ss.at[w, 0], p_rs.at[w, zl, 1 - c], here).wait_recv()

    mine_send(0)
    mine_send(1)

    def slot_of(y_, c_):
        return ((y_ // 2) * 2 + c_) * 2 + lax.rem(y_, 2)

    my_slot = slot_of(y, c)

    def row_copy(dy, dc):
        y_, c_ = lax.rem(y + dy, Y), lax.rem(c + dc, C)
        return remote(
            side.at[y_ * C + c_], rows.at[my_slot], r_ss.at[dy * 2 + dc], r_rs.at[my_slot], where_is(x, y_, z, c_)
        )

    def unseen(zh_src, odd):
        return jnp.logical_and(zh_src == 1, odd)

    def rel_copy(kv, way):
        src = side.at[pl.ds(4 * way, 4), :, pl.ds(2 * QW + kv * HD, HD)]
        return remote(src, kvrel.at[kv, way], kr_ss.at[kv, way], kr_rs.at[kv, way], where_is(x, y, z4[way], c))

    def rel_src(way):
        return z4[1 - way] // ZL

    def rel_on(kv, way):
        return [
            remote(
                kvrel.at[kv, way, i],
                kvx.at[kv, my_slot],
                kx_ss.at[kv, way * 4 + i],
                kx_rs.at[kv, my_slot],
                where_is(x, 2 * way + i // 2, z4[way], i % 2),
            )
            for i in range(4)
        ]

    def rel_start(kv):
        @pl.when(jnp.logical_not(unseen(zh, y_odd)))
        def _():
            for way in (0, 1):
                rel_copy(kv, way).start()

    def rel_pass(kv):
        for way in (0, 1):

            @pl.when(jnp.logical_not(unseen(rel_src(way), y_odd)))
            def _():
                rel_copy(kv, way).wait_recv()
                for cp in rel_on(kv, way):
                    cp.start()

    def kvx_wait(kv):
        for y_ in range(Y):
            for c_ in range(C):

                @pl.when(jnp.logical_not(unseen(1 - zh, y_ % 2 == 1)))
                def _():
                    ref = kvx.at[kv, slot_of(y_, c_)]
                    remote(ref, ref, kx_ss.at[kv, 0], kx_rs.at[kv, slot_of(y_, c_)], here).wait_recv()

    far = [(dy, dc) for dc in (0, 1) for dy in (1, 3, 2, 0) if (dy, dc) != (0, 0)]

    def y_start(*pairs):
        for dy, dc in pairs:
            row_copy(dy, dc).start()

    y_start((2, 0))
    own = pltpu.make_async_copy(side.at[head], rows.at[my_slot], r_ss.at[0])
    own.start()

    for cp in ints:
        cp.wait()
    lane = lax.broadcasted_iota(jnp.int32, (8, 128), 1)
    aux_l[...] = jnp.where(
        lane == 0,
        prompt_s[0],
        jnp.where(lane == 1, prompt_s[1], jnp.where(lane == 2, len_s[0], len_s[1])),
    )
    aux_own = pltpu.make_async_copy(aux_l, aux_v.at[c], aux_sem.at[0])
    aux_own.start()
    aux_far = remote(aux_l, aux_v.at[c], aux_sem.at[1], aux_sem.at[2], where_is(x, y, z, 1 - c))
    aux_far.start()

    def z_copy(w, way, far_, s):
        up_dev = where_is(x, y, lax.rem(z + 1 + far_, Z), c)
        down_dev = where_is(x, y, lax.rem(z + Z - 1 - far_, Z), c)
        ref = chunk(w, x, s)
        return remote(ref, ref, z_ss.at[w, way, far_, s], z_rs.at[w, s], up_dev if way == 0 else down_dev)

    def x_copy(w, way, s):
        ref, dev = chunk(w, x, s), where_is(xr if way == 0 else xl, y, z, c)
        return remote(ref, ref, x_ss.at[w, way, s], x_rs.at[w, way, s], dev)

    def x_arrived(w, way, s):
        ref = chunk(w, xl if way == 0 else xr, s)
        return remote(ref, ref, x_ss.at[w, way, s], x_rs.at[w, way, s], here)

    def x2_copy(w, way, s):
        ref, dev = chunk(w, xl if way == 0 else xr, s).at[way], where_is(xr if way == 0 else xl, y, z, c)
        return remote(ref, ref, x2_ss.at[w, way, s], x2_rs.at[w, way, s], dev)

    def x3_copy(w, s):
        ref = chunk(w, x, s)
        return remote(ref, ref, x2_ss.at[w, 0, s], x2_rs.at[w, 0, s], where_is(xo, y, z, c))

    def x3_arrived(w, s):
        ref = chunk(w, xo, s)
        return remote(ref, ref, x2_ss.at[w, 0, s], x2_rs.at[w, 0, s], here)

    def x2_arrived(w, way, s):
        ref = chunk(w, xo, s).at[way]
        return remote(ref, ref, x2_ss.at[w, way, s], x2_rs.at[w, way, s], here)

    def source(way, k):
        s = lax.rem(z + (Z - k if way == 0 else k), Z)
        return s // ZL == c, lax.rem(s, ZL)

    def x_start(w, s):
        x_copy(w, 0, s).start()
        x_copy(w, 1, s).start()

    def forwards(w, way, j, s):
        return [z_copy(w, way, i, s) for i in (2, 1, 0) if not (j == 2 and way == 1 and i == 2)]

    def stop(w, j):
        for way in (0, 1):
            live, s = source(way, 3 * j - 1 if j else 0)

            @pl.when(live)
            def _():
                if j == 1:
                    halves_wait(w, s)
                elif j == 2:
                    z_copy(w, way, 0, s).wait_recv()
                if j > 0:
                    for cp in forwards(w, way, j, s):
                        cp.start()

        for way in (0, 1):
            live, s = source(way, 3 * j - 1 if j else 0)

            @pl.when(live)
            def _():
                if j > 0 or way == 0:
                    x_start(w, s)

        for k in ((), (1,), (3, 4))[j]:
            for way in (0, 1):
                arrive(w, way, k)

    def arrive(w, way, k):
        live, s = source(way, k)

        @pl.when(live)
        def _():
            if k == 1:
                halves_wait(w, s)
            else:
                z_copy(w, way, 0, s).wait_recv()
            x_start(w, s)
            if k >= LATE:
                x3_copy(w, s).start()

    def stop_sent(w, j):
        for way in (0, 1):
            live, s = source(way, 3 * j - 1)

            @pl.when(live)
            def _():
                for cp in forwards(w, way, j, s):
                    cp.wait_send()

    def last_arrivals(w):
        for way, k in ((0, 6), (1, 6), (0, 7), (1, 7), (0, 8)):
            arrive(w, way, k)

    def pass_on(w, way, k):
        live, s = source(way, k)

        @pl.when(live)
        def _():
            for x_way in (0, 1):
                x_arrived(w, x_way, s).wait_recv()
                x2_copy(w, x_way, s).start()

    def all_on(w, low, high):
        for k in range(low, high):
            pass_on(w, 0, k)
            if 0 < k < 8:
                pass_on(w, 1, k)

    all_sources = [(way, k) for k in range(9) for way in (0, 1) if way == 0 or 0 < k < 8]

    def x2_wait(w):
        for way, k in all_sources:
            live, s = source(way, k)

            @pl.when(live)
            def _():
                if k >= LATE:
                    x_arrived(w, 0, s).wait_recv()
                    x_arrived(w, 1, s).wait_recv()
                    x3_arrived(w, s).wait_recv()
                else:
                    x2_arrived(w, 0, s).wait_recv()
                    x2_arrived(w, 1, s).wait_recv()

    mine_wait(0)
    stop(0, 0)
    y_start((1, 0))
    mine_wait(1)
    told(near_in)
    tell(far_in)
    stop(0, 1)
    stop(1, 0)
    told(far_in)
    rel_start(0)
    y_start((2, 1), (3, 0))
    stop(0, 2)
    stop(1, 1)
    rel_pass(0)
    rel_start(1)
    y_start((1, 1), (3, 1))
    all_on(0, 0, 3)
    last_arrivals(0)
    stop(1, 2)
    all_on(0, 3, LATE)
    y_start((0, 1))
    rel_pass(1)
    last_arrivals(1)
    all_on(1, 0, 3)

    for dy, dc in far:
        ref = rows.at[slot_of(lax.rem(y + dy, Y), lax.rem(c + dc, C))]
        remote(ref, ref, r_ss.at[0], r_rs.at[slot_of(lax.rem(y + dy, Y), lax.rem(c + dc, C))], here).wait_recv()
    kvx_wait(0)
    own.wait()
    aux_own.wait()
    remote(aux_l, aux_v.at[1 - c], aux_sem.at[1], aux_sem.at[2], here).wait_recv()

    to_smem = pltpu.make_async_copy(aux_v, aux_s, aux_sem.at[3])
    to_smem.start()
    to_smem.wait()

    x2_wait(0)

    def q_cols(ref, h):
        return ref.at[:, pl.ds(pl.multiple_of(h * QW, QW), QW)]

    def dq_copy(sl):
        rho = sl // 2
        y_, c_ = (rho // 2) * 2 + lax.rem(sl, 2), lax.rem(rho, 2)
        dst = q_cols(dq_out, head)
        return (
            sl == my_slot,
            remote(dqs.at[sl], dst, dq_ss.at[sl], dq_rs.at[head], where_is(x, y_, z, c_)),
            pltpu.make_async_copy(dqs.at[sl], dst, dq_ss.at[sl]),
        )

    def dkv_copy(rho, yb):
        y_, c_ = (rho // 2) * 2 + yb, lax.rem(rho, 2)
        i = dk_slot(rho, yb)
        src, dst = dkvs.at[zh, i], dkvr.at[zh, head]
        return (
            jnp.logical_and(y_ == y, c_ == c),
            remote(src, dst, dkv_ss.at[i], dkv_rs.at[zh * 8 + head], where_is(x, y_, z, c_)),
            pltpu.make_async_copy(src, dst, dkv_ss.at[i]),
        )

    def dk_slot(rho, yb):
        return (rho // 2) * 4 + yb * 2 + lax.rem(rho, 2)

    def drel_copy(kv, way, yb):
        dev = where_is(x, y, jnp.where(way == 0, z4[0], z4[1]), c)
        src = dkvs.at[1 - zh, pl.ds(way * 4 + yb * 2, 2), kv]
        return remote(src, dkrel.at[kv, way, yb], dr_ss.at[kv, way, yb], dr_rs.at[kv, way, yb], dev)

    def drel_start(kv, way):
        drel_copy(kv, way, 0).start()

        @pl.when(zh == 1)
        def _():
            drel_copy(kv, way, 1).start()

    def drel_on(kv, way, yb):
        zs = rel_src(way)
        return [
            remote(
                dkrel.at[kv, way, yb, i],
                dkvr.at[zs, head, kv],
                df_ss.at[kv, way, yb * 2 + i],
                df_rs.at[kv, head],
                where_is(x, 2 * way + yb, z4[way], i),
            )
            for i in (0, 1)
        ]

    def drel_pass(kv, way):
        drel_copy(kv, way, 0).wait_recv()
        for cp in drel_on(kv, way, 0):
            cp.start()

        @pl.when(rel_src(way) == 1)
        def _():
            drel_copy(kv, way, 1).wait_recv()
            for cp in drel_on(kv, way, 1):
                cp.start()

    def send(copies):
        local, far_cp, near_cp = copies

        @pl.when(local)
        def _():
            near_cp.start()

        @pl.when(jnp.logical_not(local))
        def _():
            far_cp.start()

    def sent(copies):
        local, far_cp, near_cp = copies

        @pl.when(local)
        def _():
            near_cp.wait()

        @pl.when(jnp.logical_not(local))
        def _():
            far_cp.wait_send()

    def fold(a, op):
        return op(a.reshape(CHUNK // 8, 8, ROWS), 0)

    def keys_of(kv, prompt, rho, to):
        to[:PLEN] = prefix[kv][prompt].reshape(PLEN, HD)
        for b in (0, 1):
            i = rho * 2 + b
            near = pl.ds(pl.multiple_of(PLEN + (2 * b + zh) * TOK, TOK), TOK)
            over = pl.ds(pl.multiple_of(PLEN + (2 * b + 1 - zh) * TOK, TOK), TOK)
            low = 2 * QW + kv * HD
            to[near] = rows[i, :, low : low + HD]
            crossed = kvx[kv, i].astype(F32)
            if b == 1:
                crossed = jnp.where(zh == 1, crossed, 0.0)
            to[over] = crossed.astype(BF16)

    def leave(kv, rho, grad):
        for i in range(4):
            for ct in (0, 1):
                low = (i * 2 + ct) * 64
                term[kv, rho, ct, i] = grad[low : low + 64].astype(BF16)
        for tb in range(4):
            low = PLEN + tb * TOK
            dkvs[tb % 2, dk_slot(rho, tb // 2), kv] = grad[low : low + TOK].astype(BF16)

    def weigh(rho, carry):
        prompt = aux_s[lax.rem(rho, 2), 0, rho // 2]
        length = aux_s[lax.rem(rho, 2), 0, 2 + rho // 2]
        k_rho = kk.at[rho]
        keys_of(0, prompt, rho, k_rho)
        acc = []
        for b in (0, 1):
            i = rho * 2 + b
            qa, ga = rows[i, :, :QW], rows[i, :, QW : 2 * QW]
            tok = lax.broadcasted_iota(jnp.int32, (TOK, HD), 0) + (64 * b + TOK * zh)
            keep = jnp.where(tok < length, 1.0, 0.0)
            q = jnp.concatenate([qa[:, h * HD : (h + 1) * HD] for h in range(REP)], axis=0)
            g = jnp.concatenate(
                [(ga[:, h * HD : (h + 1) * HD].astype(F32) * keep).astype(BF16) for h in range(REP)], axis=0
            )
            qh[i] = q
            gh[i] = g
            top = jnp.full((8, ROWS), -jnp.inf, F32)
            for n in range(CHUNKS):
                at = slice(n * CHUNK, (n + 1) * CHUNK)
                s = dot_nt(k_rho[at], q)
                if n == CHUNKS - 1:
                    col = lax.broadcasted_iota(jnp.int32, (CHUNK, ROWS), 1)
                    key = lax.broadcasted_iota(jnp.int32, (CHUNK, ROWS), 0)
                    s = jnp.where(key <= lax.rem(col, TOK) + (64 * b + TOK * zh), s, -jnp.inf)
                s_scr[b, at] = s
                top = jnp.maximum(top, fold(s, jnp.max))
            top = jnp.max(top, 0, keepdims=True)
            total = jnp.zeros((8, ROWS), F32)
            for n in range(CHUNKS):
                at = slice(n * CHUNK, (n + 1) * CHUNK)
                e = jnp.exp2((s_scr[b, at] - top) * SCALE2)
                s_scr[b, at] = e
                total = total + fold(e, jnp.sum)
            inv = 1.0 / jnp.sum(total, 0, keepdims=True)
            for n in range(CHUNKS):
                at = slice(n * CHUNK, (n + 1) * CHUNK)
                p = s_scr[b, at] * inv
                p_scr[i, at] = p
                b_scr[b, at] = p.astype(BF16)
            acc.append(dot_nn(b_scr[b], g))
        leave(1, rho, acc[0] + acc[1])

        @pl.when(lax.rem(rho, 2) == 1)
        def _():
            drel_start(1, rho // 2)

        @pl.when(rho == 0)
        def _():
            all_on(1, 3, LATE)

        return carry

    def differentiate(rho, carry):
        prompt = aux_s[lax.rem(rho, 2), 0, rho // 2]
        keys_of(1, prompt, rho, vv)
        acc = []
        for b in (0, 1):
            i = rho * 2 + b
            mixed = jnp.zeros((8, ROWS), F32)
            for n in range(CHUNKS):
                at = slice(n * CHUNK, (n + 1) * CHUNK)
                dp = dot_nt(vv[at], gh[i])
                dp_scr[b, at] = dp
                mixed = mixed + fold(p_scr[i, at] * dp, jnp.sum)
            delta = jnp.sum(mixed, 0, keepdims=True)
            for n in range(CHUNKS):
                at = slice(n * CHUNK, (n + 1) * CHUNK)
                ds_scr[i, at] = (p_scr[i, at] * (dp_scr[b, at] - delta)).astype(BF16)
            acc.append(dot_nn(ds_scr[i], qh[i]))
        leave(0, rho, (acc[0] + acc[1]) * SCALE)

        @pl.when(lax.rem(rho, 2) == 1)
        def _():
            drel_start(0, rho // 2)

        for b in (0, 1):
            send(dkv_copy(rho, b))

        @pl.when(rho == 2)
        def _():
            for way in (0, 1):
                drel_pass(1, way)

        first(1, order(rho))

        @pl.when(rho >= 2)
        def _():
            second(1, order(rho - 2))

        return carry

    def query_grads(rho, carry):
        for b in (0, 1):
            i = rho * 2 + b
            dq = (dot_tn(kk[rho], ds_scr[i]) * SCALE).T.astype(BF16)
            for h in range(REP):
                dqs[i, :, h * HD : (h + 1) * HD] = dq[h * TOK : (h + 1) * TOK]
        return carry

    def part(w, x_, n, half):
        return dense.at[w, x_ * 2 + n // 2, half, pl.ds(lax.rem(n, 2) * 2, 2)]

    def own_part(w, x_, n, half):
        return dense[w, x_ * 2 + n // 2, half, pl.ds(lax.rem(n, 2) * 2, 2)].astype(F32)

    def rx_copy(w, way, n):
        if way == 0:
            src, dst, dev = part(w, xo, n, 0), ra.at[w, n], where_is(xr, y, z, c)
        elif way == 1:
            src, dst, dev = part(w, xo, n, 1), rb.at[w, n], where_is(xl, y, z, c)
        elif way == 2:
            src, dst, dev = part(w, xr, n, 1), rb1.at[w, n], where_is(xr, y, z, c)
        else:
            src, dst, dev = part(w, xl, n, 0), ra1.at[w, n], where_is(xl, y, z, c)
        return remote(src, dst, rx_ss.at[w, way, n], rx_rs.at[w, way, n], dev)

    def rx2_copy(w, way, n):
        if way == 0:
            src, dst, dev = ra.at[w, n], ra2.at[w, n], where_is(xr, y, z, c)
        else:
            src, dst, dev = rb.at[w, n], rb2.at[w, n], where_is(xl, y, z, c)
        return remote(src, dst, rx2_ss.at[w, way, n], rx2_rs.at[w, way, n], dev)

    rising = (zh != c) == (zl < 4)

    def order(i):
        n = lax.rem(i, 2) * 2 + i // 2
        return jnp.where(rising, n, 3 - n)

    def spread_all(w):
        def spread_half(i, carry):
            ip = jnp.where(rising, i, 1 - i)
            two = pl.ds(ip * 2, 2)

            def spread(p, carry):
                acc = jnp.zeros((2, 2, 64, HD), F32)
                for rho in range(4):
                    hit = aux_s[rho % 2, 0, rho // 2] == p
                    acc = acc + jnp.where(hit, term[w, rho, :, two].astype(F32), 0.0)
                dense[w, p, :, two] = acc.astype(BF16)
                return carry

            lax.fori_loop(0, PROMPTS, spread, 0)
            for j in (0, 1):
                for way in (0, 1):
                    rx_copy(w, way, order(2 * i + j)).start()
            return carry

        lax.fori_loop(0, 2, spread_half, 0)

    def z_dist(zt):
        return lax.rem(c * ZL + zt - z + 23, Z) - 7

    def z_direct(w, zt, ct, d):
        src, dst, zd = xsum.at[w, zt, ct], zr.at[w, d + 4], c * ZL + zt
        return (
            jnp.logical_and(d == 0, ct == c),
            remote(src, dst, rz_ss.at[w, ct, zt], rz_rs.at[w, d + 4], where_is(x, y, zd, ct)),
            pltpu.make_async_copy(src, dst, rz_ss.at[w, ct, zt]),
        )

    def z_stop(w, zt, d):
        up_ = d > 0
        zd = lax.rem(z + Z + jnp.where(up_, d - 4, d + 4), Z)
        i = jnp.where(up_, d, -d) - 5
        return remote(xsum.at[w, zt], zrel.at[w, i], rz_ss.at[w, 0, zt], rl_rs.at[w, i], where_is(x, y, zd, c))

    def is_far(d):
        return jnp.logical_or(d > 4, d < -4)

    def is_near(d):
        return jnp.logical_and(d < 4, d > -4)

    def first(w, n):
        rx_copy(w, 0, n).wait_recv()
        ra[w, n] = (ra[w, n].astype(F32) + own_part(w, xr, n, 0)).astype(BF16)
        rx2_copy(w, 0, n).start()
        rx_copy(w, 1, n).wait_recv()
        rb[w, n] = (rb[w, n].astype(F32) + own_part(w, xl, n, 1)).astype(BF16)
        rx2_copy(w, 1, n).start()
        rx_copy(w, 2, n).start()
        rx_copy(w, 3, n).start()

    def second(w, n):
        rx_copy(w, 3, n).wait_recv()
        rx2_copy(w, 0, n).wait_recv()
        one = own_part(w, x, n, 0) + ra1[w, n].astype(F32) + ra2[w, n].astype(F32)
        rx_copy(w, 2, n).wait_recv()
        rx2_copy(w, 1, n).wait_recv()
        two = own_part(w, x, n, 1) + rb1[w, n].astype(F32) + rb2[w, n].astype(F32)
        for i in (0, 1):
            zt = 2 * n + i
            xsum[w, zt, 0] = one[i].astype(BF16)
            xsum[w, zt, 1] = two[i].astype(BF16)
            d = z_dist(zt)

            @pl.when(is_near(d))
            def _():
                for ct in (0, 1):
                    send(z_direct(w, zt, ct, d))

            @pl.when(is_far(d))
            def _():
                z_stop(w, zt, d).start()

    zt_stop = lax.rem(zl + 4, ZL)
    d_stop = z_dist(zt_stop)

    def stop_sum(w):
        def stop_wait(i, carry):
            @pl.when(jnp.logical_or(i < 3, d_stop > 0))
            def _():
                remote(zrel.at[w, i], zrel.at[w, i], rz_ss.at[w, 0, 0], rl_rs.at[w, i], here).wait_recv()

            return carry

        lax.fori_loop(0, 4, stop_wait, 0)
        for ct in (0, 1):
            three = xsum[w, zt_stop, ct].astype(F32)
            for i in range(3):
                three = three + zrel[w, i, ct].astype(F32)

            @pl.when(d_stop > 0)
            def _():
                xsum[w, zt_stop, ct] = (three + zrel[w, 3, ct].astype(F32)).astype(BF16)

            @pl.when(d_stop < 0)
            def _():
                xsum[w, zt_stop, ct] = three.astype(BF16)

            z_direct(w, zt_stop, ct, d_stop)[1].start()

    lax.fori_loop(0, 4, weigh, 0)
    spread_all(1)
    x2_wait(1)
    kvx_wait(1)
    lax.fori_loop(0, 4, differentiate, 0)
    spread_all(0)
    drel_pass(0, 0)
    lax.fori_loop(0, 4, query_grads, 0)

    def last(i, carry):
        @pl.when(i < 4)
        def _():
            first(0, order(i))
            send(dq_copy(2 * i))
            send(dq_copy(2 * i + 1))

        @pl.when(i < 2)
        def _():
            second(1, order(i + 2))

        @pl.when(i == 1)
        def _():
            drel_pass(0, 1)

        @pl.when(i == 2)
        def _():
            stop_sum(1)

        @pl.when(i >= 1)
        def _():
            second(0, order(i - 1))

        return carry

    lax.fori_loop(0, 5, last, 0)
    stop_sum(0)

    def dkv_wait(h, carry):
        near = dkvr.at[zh, h]

        @pl.when(h != head)
        def _():
            remote(near, near, dkv_ss.at[0], dkv_rs.at[zh * 8 + h], here).wait_recv()

        @pl.when(jnp.logical_not(unseen(zh, y_odd)))
        def _():
            for kv in (0, 1):
                over = dkvr.at[1 - zh, h, kv]
                remote(over, over, dkv_ss.at[0], df_rs.at[kv, h], here).wait_recv()

        return carry

    def dkv_sent(i, carry):
        for yb in (0, 1):
            sent(dkv_copy(i, yb))
        return carry

    lax.fori_loop(0, 4, dkv_sent, 0)
    lax.fori_loop(0, 8, dkv_wait, 0)
    def z_sent(i, carry):
        w, n = i // ZL, lax.rem(i, ZL)
        d = z_dist(n)

        @pl.when(is_far(d))
        def _():
            z_stop(w, n, d).wait_send()

        @pl.when(jnp.logical_not(is_far(d)))
        def _():
            for ct in (0, 1):
                sent(z_direct(w, n, ct, d))

        return carry

    def z_wait(i, carry):
        for w in (0, 1):

            @pl.when(jnp.logical_not(jnp.logical_and(own_core, i == 4)))
            def _():
                remote(zr.at[w, i], zr.at[w, i], rz_ss.at[w, 0, 0], rz_rs.at[w, i], here).wait_recv()

        return carry

    lax.fori_loop(0, 2 * ZL, z_sent, 0)
    lax.fori_loop(0, 9, z_wait, 0)

    def dq_wait(h, carry):
        @pl.when(h != head)
        def _():
            ref = q_cols(dq_out, h)
            remote(ref, ref, dq_ss.at[0], dq_rs.at[h], here).wait_recv()

        return carry

    def dq_sent(i, carry):
        sent(dq_copy(i))
        return carry

    lax.fori_loop(0, 8, dq_sent, 0)
    lax.fori_loop(0, 8, dq_wait, 0)
    aux_far.wait_send()
    for dy, dc in far:
        row_copy(dy, dc).wait_send()

    @pl.when(jnp.logical_not(unseen(zh, y_odd)))
    def _():
        for kv in (0, 1):
            for way in (0, 1):
                rel_copy(kv, way).wait_send()

    for way in (0, 1):

        @pl.when(jnp.logical_not(unseen(rel_src(way), y_odd)))
        def _():
            for cp in rel_on(0, way) + rel_on(1, way):
                cp.wait_send()

        for kv in (0, 1):
            drel_copy(kv, way, 0).wait_send()
            for cp in drel_on(kv, way, 0):
                cp.wait_send()

        @pl.when(zh == 1)
        def _():
            for kv in (0, 1):
                drel_copy(kv, way, 1).wait_send()

        @pl.when(rel_src(way) == 1)
        def _():
            for kv in (0, 1):
                for cp in drel_on(kv, way, 1):
                    cp.wait_send()

    for w in (0, 1):
        for i in (1, 2, 3, 4):
            mine_far(w, i).wait_send()

        @pl.when(jnp.logical_not(own_core))
        def _():
            mine_far(w, 0).wait_send()

    for w in (0, 1):
        for j in (1, 2):
            stop_sent(w, j)

    def x_sent(s, carry):
        for w in (0, 1):
            for way in (0, 1):
                x_copy(w, way, s).wait_send()
        return carry

    lax.fori_loop(0, ZL, x_sent, 0)
    for w in (0, 1):
        for way, k in all_sources:
            live, s = source(way, k)

            @pl.when(live)
            def _():
                if k >= LATE:
                    x3_copy(w, s).wait_send()
                else:
                    x2_copy(w, 0, s).wait_send()
                    x2_copy(w, 1, s).wait_send()

    def rx_sent(n, carry):
        for w in (0, 1):
            for way in range(4):
                rx_copy(w, way, n).wait_send()
            for way in (0, 1):
                rx2_copy(w, way, n).wait_send()
        return carry

    lax.fori_loop(0, 4, rx_sent, 0)


def finish(dq_in, dkvr_in, zr_in, dq_out, dk_out, dv_out, gpk_out, gpv_out, dq, dkvr, zr, sem):
    loads = [
        pltpu.make_async_copy(dq_in, dq, sem.at[0]),
        pltpu.make_async_copy(dkvr_in, dkvr, sem.at[1]),
        pltpu.make_async_copy(zr_in, zr, sem.at[2]),
    ]
    for cp in loads:
        cp.start()
    loads[0].wait()
    store = pltpu.make_async_copy(dq, dq_out, sem.at[3])
    store.start()
    loads[1].wait()
    loads[2].wait()
    t = lax.axis_index("tp")
    near = lax.rem(t, ZH)
    whole = jnp.where(jnp.logical_and(near == 1, lax.rem(t // ZH, 2) == 1), 0, 1)
    for h in range(8):
        over = jnp.where(whole == 1, dkvr[1 - near, h].astype(F32), 0.0)
        summed = dkvr[near, h].astype(F32) + over
        dk_out[:, h * HD : (h + 1) * HD] = summed[0].astype(BF16)
        dv_out[:, h * HD : (h + 1) * HD] = summed[1].astype(BF16)
    for w, ref in ((0, gpk_out), (1, gpv_out)):
        all_z = zr[w, 0].astype(F32)
        for i in range(1, 9):
            all_z = all_z + zr[w, i].astype(F32)
        ref[...] = all_z.astype(BF16)
    store.wait()


def body(queries, keys, values, out_grad, prefix_keys, prefix_values, lengths, prompt_of):
    dma = pltpu.SemaphoreType.DMA
    vm = lambda *shape: pltpu.VMEM(shape, BF16)
    out = lambda *shape: jax.ShapeDtypeStruct(shape, BF16)
    hbm = pl.BlockSpec(memory_space=pl.ANY)
    vmem = pl.BlockSpec(memory_space=pltpu.VMEM)
    wide = 2 * QW + 2 * HD
    dq, dkvr, zr = pl.pallas_call(
        kernel,
        out_shape=(out(TOK, 8 * REP * HD), out(2, 8, 2, TOK, HD), out(2, 9, 64, HD)),
        in_specs=[hbm] * 8,
        out_specs=(hbm,) * 3,
        scratch_shapes=[
            pltpu.SMEM((2,), jnp.int32),
            pltpu.SMEM((2,), jnp.int32),
            pltpu.VMEM((8, 128), jnp.int32),
            pltpu.VMEM((2, 8, 128), jnp.int32),
            pltpu.SMEM((2, 8, 128), jnp.int32),
            vm(TOK, 8 * QW),
            vm(TOK, 8 * QW),
            vm(TOK, 8 * HD),
            vm(TOK, 8 * HD),
            vm(8, TOK, wide),
            vm(2, 2, 4, TOK, HD),
            vm(8, TOK, wide),
            vm(2, 8, TOK, HD),
            vm(8, 4, 2, 64, HD),
            vm(8, 4, 2, 64, HD),
            vm(2, 4, 2, 4, 64, HD),
            vm(2, 8, 2, 4, 64, HD),
            vm(8, TOK, REP * HD),
            vm(2, 8, 2, TOK, HD),
            vm(2, 2, 2, 2, TOK, HD),
            vm(2, 4, 2, 64, HD),
            vm(2, 4, 2, 64, HD),
            vm(2, 4, 2, 64, HD),
            vm(2, 4, 2, 64, HD),
            vm(2, 4, 2, 64, HD),
            vm(2, 4, 2, 64, HD),
            vm(2, 8, 2, 64, HD),
            vm(2, 4, 2, 64, HD),
            vm(8, ROWS, HD),
            vm(8, ROWS, HD),
            vm(4, PLEN + RCAP, HD),
            vm(PLEN + RCAP, HD),
            pltpu.VMEM((2, PLEN + RCAP, ROWS), F32),
            pltpu.VMEM((2, PLEN + RCAP, ROWS), F32),
            pltpu.VMEM((8, PLEN + RCAP, ROWS), F32),
            vm(2, PLEN + RCAP, ROWS),
            vm(8, PLEN + RCAP, ROWS),
            dma((4,)),
            dma((4,)), dma((8,)), dma((8,)), dma((2, 2)), dma((2, 2)), dma((2, 8)), dma((2, 8)),
            pltpu.SemaphoreType.REGULAR((2,)), pltpu.SemaphoreType.REGULAR((2,)),
            dma((2, 5)), dma((2, 8, 2)),
            dma((2, 2, 3, 8)), dma((2, 8)), dma((2, 2, 8)), dma((2, 2, 8)), dma((2, 2, 8)), dma((2, 2, 8)),
            dma((8,)), dma((8,)), dma((8,)), dma((16,)), dma((2, 2, 2)), dma((2, 2, 2)), dma((2, 2, 4)), dma((2, 8)),
            dma((2, 4, 4)), dma((2, 4, 4)), dma((2, 2, 4)), dma((2, 2, 4)),
            dma((2, 2, 8)), dma((2, 9)), dma((2, 4)),
        ],
        compiler_params=pltpu.CompilerParams(
            collective_id=0, has_side_effects=True, vmem_limit_bytes=62 * 1024 * 1024
        ),
        cost_estimate=pl.CostEstimate(flops=2_000_000_000, bytes_accessed=4_000_000, transcendentals=1_400_000),
    )(queries, keys, values, out_grad, prefix_keys, prefix_values, lengths, prompt_of)
    return pl.pallas_call(
        finish,
        out_shape=(
            jax.ShapeDtypeStruct(queries.shape, BF16),
            jax.ShapeDtypeStruct(keys.shape, BF16),
            jax.ShapeDtypeStruct(values.shape, BF16),
            jax.ShapeDtypeStruct(prefix_keys.shape, BF16),
            jax.ShapeDtypeStruct(prefix_values.shape, BF16),
        ),
        in_specs=[hbm] * 3,
        out_specs=(hbm,) + (vmem,) * 4,
        scratch_shapes=[vm(TOK, 8 * REP * HD), vm(2, 8, 2, TOK, HD), vm(2, 9, 64, HD), dma((4,))],
        compiler_params=pltpu.CompilerParams(vmem_limit_bytes=62 * 1024 * 1024),
        name="finish",
    )(dq, dkvr, zr)


def solution(mesh):
    in_specs = (
        P(("resp", "tp"), None),
        P(("resp", "tp"), None),
        P(("resp", "tp"), None),
        P(("resp", "tp"), None),
        P("resp", "tp"),
        P("resp", "tp"),
        P("resp"),
        P("resp"),
    )
    out_specs = (
        P(("resp", "tp"), None),
        P(("resp", "tp"), None),
        P(("resp", "tp"), None),
        P("resp", "tp"),
        P("resp", "tp"),
    )
    return jax.shard_map(body, mesh=mesh, in_specs=in_specs, out_specs=out_specs, check_vma=False)
```
